512 devices in a mesh: span: 8 (over y_lo, core), seq: 32 (over x, z), rep: 2 (over y_hi).
Axes of the slice: x: 4, y: 8 (y_hi: 2, y_lo: 4; y = y_hi * 4 + y_lo), z: 8, core: 2. Of those that a mesh axis runs over, the one named last changes fastest.
Arguments:
- queries: bfloat16 [16, 512, 4096], P(('rep', 'span'), 'seq'), parts along dimension 0, may hold values from -5 to 5
- keys: bfloat16 [16, 512, 4096], P(('rep', 'span'), 'seq'), parts along dimension 0, may hold values from -5 to 5
- values: bfloat16 [16, 512, 4096], P(('rep', 'span'), 'seq'), parts along dimension 0, may hold values from -6 to 6
- timesteps: int32 [16], P(('rep', 'span')), parts along dimension 0, may hold values from 0 to 999
- history: int32 [16, 256], P(('rep', 'span')), parts along dimension 0, may hold values from 0 to 1, as said below
- gate_weight: bfloat16 [256, 4096], P(None, 'seq'), may hold values from -0.375 to 0.375
Outputs:
- gated: bfloat16 [16, 512, 4096], P(('rep', 'span'), 'seq'), parts along dimension 0
The draws below stay inside these ranges and needn't reach their ends.
There are 2 independent parts, one for each index of `rep`. The reference program is written for one: setup_inputs(seed, part) draws one part's arguments, and reference() takes and returns one part's arrays. A program takes and returns all parts, laid end to end along the dimension named above; an argument that names none is the same for every part. Nothing has to cross between parts.
Inputs may be any that keep to these rules, and one draw needn't show every extreme that they name: history[c, j * 32 + b] is 0 wherever j >= c; for c >= 1, history[c, (c - 1) * 32] is 1.
All inputs are finite; a program needn't handle non-finite values.
Results may differ from the reference program's by a relative error of at most 0.005.
Values may be sent and summed in bfloat16 or wider, within the bound.
A program may use at most 64 MiB of HBM per device.

```python
import math
import jax
import jax.numpy as jnp
from jax import lax

HEADS = 32
HD = 128
FREQ = 256
STEPS = 1000
TOK_DEV = 16
TOKC = 512
SPANS = 8
N_SEQ = 32


def draw_queries(key, part):
    key = jax.random.fold_in(key, 11)
    base = 1.6 * jax.random.truncated_normal(key, -3.0, 3.0, (SPANS, TOKC, HEADS * HD), jnp.float32)
    return base.astype(jnp.bfloat16)


def draw_keys(key, part):
    key = jax.random.fold_in(key, 12)
    base = 1.6 * jax.random.truncated_normal(key, -3.0, 3.0, (SPANS, TOKC, HEADS * HD), jnp.float32)
    return base.astype(jnp.bfloat16)


def draw_history(key, part):
    key = jax.random.fold_in(key, 37)
    wide = jax.random.randint(key, (SPANS, SPANS * N_SEQ), 0, 1048576, dtype=jnp.int32)
    bits = (wide % 2).astype(jnp.int32)
    rowpos = jnp.arange(SPANS, dtype=jnp.int32)[:, None]
    colpos = jnp.arange(SPANS * N_SEQ, dtype=jnp.int32)[None, :]
    colchunk = colpos // N_SEQ
    forced = colpos == (rowpos - 1) * N_SEQ
    bits = jnp.where(forced, jnp.int32(1), bits)
    return jnp.where(colchunk < rowpos, bits, jnp.int32(0)).astype(jnp.int32)


def touch_ends(result, rng, low, top_value):
    shape = result.shape
    index_at = [jax.random.randint(jax.random.fold_in(rng, axis), (), 0, shape[axis]) for axis in range(len(shape))]
    result = result.at[tuple(index_at)].set(low)
    longest = shape.index(max(shape))
    index_at[longest] = (index_at[longest] + 1) % shape[longest]
    return result.at[tuple(index_at)].set(top_value)


def levels(own_key, dims, cuts, least, high):
    loudness, own = 1.0, jax.random.fold_in(own_key, 6)
    for position, shards_of in cuts:
        steps = jnp.exp(jax.random.uniform(jax.random.fold_in(own, position), (shards_of,), jnp.float32, least / len(cuts), high / len(cuts)))
        loudness = loudness * jnp.repeat(steps, dims[position] // shards_of).reshape([-1 if axis == position else 1 for axis in range(len(dims))])
    return loudness


def bell_draw(rng, shape, width, bound, split=(), kind=jnp.bfloat16):
    entries = jax.random.normal(rng, shape, jnp.float32) * width
    if len(split) > 0:
        entries = levels(rng, shape, split, -0.22, 0.18) * entries
    return jnp.clip(entries, min=-bound, max=bound).astype(kind)


def setup_inputs(seed: int = 0, part: int = 0) -> dict:
    key_of = jax.random.split(jax.random.key(seed), 7)
    part_keys = jax.random.split(jax.random.fold_in(key_of[6], part), 7)
    queries = draw_queries(jax.random.fold_in(jax.random.fold_in(key_of[6], part), 71), part)
    keys = draw_keys(jax.random.fold_in(jax.random.fold_in(key_of[6], part), 71), part)
    values = bell_draw(part_keys[2], (SPANS, TOKC, HEADS * HD), 1.0, 6.0, ((0, 8), (1, 32)))
    timesteps = touch_ends(jax.random.randint(part_keys[3], (SPANS,), 0, STEPS), jax.random.fold_in(part_keys[3], 1), 0, STEPS - 1).astype(jnp.int32)
    history = draw_history(jax.random.fold_in(jax.random.fold_in(key_of[6], part), 71), part)
    gate_weight = bell_draw(key_of[5], (FREQ, HEADS * HD), FREQ ** -0.5, 0.375, ((1, 32),))
    return dict(queries=queries, keys=keys, values=values, timesteps=timesteps, history=history, gate_weight=gate_weight)


def embed(steps):
    half = FREQ // 2
    freqs = jnp.exp(-math.log(10000.0) * jnp.arange(half, dtype=jnp.float32) / half)
    angle = steps.astype(jnp.float32)[:, None] * freqs[None, :]
    return jnp.concatenate([jnp.cos(angle), jnp.sin(angle)], axis=-1)

def reference(queries, keys, values, timesteps, history, gate_weight):
    gate = jnp.dot(embed(timesteps).astype(jnp.bfloat16), gate_weight, preferred_element_type=jnp.float32)
    blocks = history.reshape(SPANS, SPANS, N_SEQ)
    own = jnp.eye(SPANS, dtype=jnp.int32)[:, :, None]
    visible = blocks + own > 0
    scale = 1.0 / math.sqrt(HD)
    key_heads = keys.reshape(SPANS * TOKC, HEADS, HD).transpose(1, 0, 2)
    value_heads = values.reshape(SPANS * TOKC, HEADS, HD).transpose(1, 0, 2)
    results = []
    for span in range(SPANS):
        keymask = jnp.repeat(visible[span].reshape(SPANS * N_SEQ), TOK_DEV)
        query_heads = queries[span].reshape(TOKC, HEADS, HD).transpose(1, 0, 2)

        def one_head(operands):
            query_h, key_h, value_h = operands
            scores = jnp.dot(query_h, key_h.T, preferred_element_type=jnp.float32) * scale
            scores = jnp.where(keymask[None, :], scores, -jnp.inf)
            largest = lax.optimization_barrier(jnp.max(scores, axis=-1, keepdims=True))
            weights = jnp.exp(scores - largest)
            total = lax.optimization_barrier(jnp.sum(weights, axis=-1, keepdims=True))
            summed = jnp.dot(weights.astype(jnp.bfloat16), value_h, preferred_element_type=jnp.float32)
            return summed / total
        attended = lax.map(one_head, (query_heads, key_heads, value_heads))
        attended = attended.transpose(1, 0, 2).reshape(TOKC, HEADS * HD)
        results.append((attended * gate[span][None, :]).astype(jnp.bfloat16))
    return jnp.stack(results, axis=0)
```

```python
import functools
import math

import jax
import jax.numpy as jnp
from jax import lax
from jax.experimental import pallas as pl
from jax.experimental.pallas import tpu as pltpu
from jax.sharding import PartitionSpec as P

HD = 128
FREQ = 256
RAISE = math.log2(math.e) / math.sqrt(HD)
HIDDEN = -1e30


def kernel(
    n_span, n_x, n_z, tok,
    q_hbm, k_hbm, v_hbm, steps_ref, history_ref, gatew_ref,
    out_ref,
    q_in, k_in, v_in, kv_stage, q_stage, kv, qbuf, obuf, bias, gate_row, top, total, accum,
    in_sem, kv_recv, kv_send, q_recv, q_send, down_send, side_send, o_recv, o_send,
):
    n_seq = n_x * n_z
    rows = n_z * tok
    n_chip = n_span // 2
    span, seq = lax.axis_index("span"), lax.axis_index("seq")
    chip, core = span // 2, lax.rem(span, 2)
    x, z = seq // n_z, lax.rem(seq, n_z)
    x_off = [0, 1, 3, 2] if n_x == 4 else list(range(n_x))

    def z_off(r):
        return jnp.where(lax.rem(r, 2) == 1, (r + 1) // 2, n_z - r // 2)

    def ahead(g, r):
        return lax.rem(x + x_off[g], n_x) * n_z + lax.rem(z + z_off(r), n_z)

    def behind(g, r):
        return lax.rem(x + n_x - x_off[g], n_x) * n_z + lax.rem(z + 2 * n_z - z_off(r), n_z)

    fetch = [
        pltpu.make_async_copy(src.at[0], dst, in_sem.at[i])
        for i, (src, dst) in enumerate(((k_hbm, k_in), (v_hbm, v_in), (q_hbm, q_in)))
    ]
    for copy in fetch:
        copy.start()
    barrier = pltpu.get_barrier_semaphore()

    @pl.loop(1, n_seq)
    def _(d):
        pl.semaphore_signal(barrier, inc=1, device_id={"seq": lax.rem(seq + d, n_seq)})

    sibling = span + 1 - 2 * core
    pl.semaphore_signal(barrier, inc=1, device_id={"span": sibling})

    @pl.when(chip > 0)
    def _():
        pl.semaphore_signal(barrier, inc=1, device_id={"span": span - 2})

    @pl.when(chip < n_chip - 1)
    def _():
        pl.semaphore_signal(barrier, inc=1, device_id={"span": span + 2})

    fetch[0].wait()
    for t in range(n_seq):
        kv_stage[t, 0] = k_in[:, t * HD : (t + 1) * HD]
    fetch[1].wait()
    for t in range(n_seq):
        kv_stage[t, 1] = v_in[:, t * HD : (t + 1) * HD]
    fetch[2].wait()
    for t in range(n_seq):
        q_stage[t] = q_in[:, t * HD : (t + 1) * HD]

    kv[span, 0, :, 0:tok, :] = kv_stage[seq]
    qbuf[0, 0:tok, :] = q_stage[seq]

    others = n_seq + (chip > 0).astype(jnp.int32) + (chip < n_chip - 1).astype(jnp.int32)
    pl.semaphore_wait(barrier, others)

    for g in range(n_x):

        @pl.loop(1 if g == 0 else 0, n_z)
        def _(r):
            to = ahead(g, r)
            pltpu.make_async_remote_copy(
                src_ref=kv_stage.at[to],
                dst_ref=kv.at[span, g, :, pl.ds(pl.multiple_of(r * tok, tok), tok), :],
                send_sem=kv_send,
                recv_sem=kv_recv.at[span, g],
                device_id={"seq": to},
            ).start()

    for g in range(n_x):

        @pl.loop(1 if g == 0 else 0, n_z)
        def _(r):
            to = ahead(g, r)
            pltpu.make_async_remote_copy(
                src_ref=q_stage.at[to],
                dst_ref=qbuf.at[g, pl.ds(pl.multiple_of(r * tok, tok), tok), :],
                send_sem=q_send,
                recv_sem=q_recv,
                device_id={"seq": to},
            ).start()

    half = FREQ // 2
    k_index = lax.broadcasted_iota(jnp.int32, (8, half), 1).astype(jnp.float32)
    freqs = jnp.exp(-math.log(10000.0) * k_index / half)
    angle = steps_ref[0].astype(jnp.float32) * freqs
    embedding = jnp.concatenate([jnp.cos(angle), jnp.sin(angle)], axis=-1).astype(jnp.bfloat16)
    gate_row[...] = jnp.dot(embedding, gatew_ref[...], preferred_element_type=jnp.float32)

    n_block = n_span * n_seq
    spread = jnp.where(
        lax.broadcasted_iota(jnp.int32, (n_span, n_block), 1) // n_seq
        == lax.broadcasted_iota(jnp.int32, (n_span, n_block), 0),
        history_ref[...],
        0,
    ).astype(jnp.float32).astype(jnp.bfloat16)
    key_at = lax.broadcasted_iota(jnp.int32, (1, n_seq * tok), 1)
    key_g, key_r = key_at // rows, lax.rem(key_at, rows) // tok
    key_dx = jnp.where(key_g == 2, 3, jnp.where(key_g == 3, 2, key_g)) if n_x == 4 else key_g
    key_block = lax.rem(x + n_x - key_dx, n_x) * n_z + lax.rem(z + 2 * n_z - z_off(key_r), n_z)
    place = lax.rem(lax.broadcasted_iota(jnp.int32, (n_block, n_seq * tok), 0), n_seq) == key_block
    shown = jnp.dot(
        spread, jnp.where(place, 1.0, 0.0).astype(jnp.bfloat16), preferred_element_type=jnp.float32
    )
    own = lax.broadcasted_iota(jnp.int32, shown.shape, 0) == span
    bias[...] = jnp.where(own | (shown > 0.5), 0.0, HIDDEN)

    def chunk_copy(j, g, sems, to):
        return pltpu.make_async_remote_copy(
            src_ref=kv.at[j, g],
            dst_ref=kv.at[j, g],
            send_sem=sems.at[j, g],
            recv_sem=kv_recv.at[j, g],
            device_id={"span": to},
        )

    def pass_on(j, g):
        @pl.when(chip < n_chip - 1)
        def _():
            chunk_copy(j, g, down_send, span + 2).start()

    def pass_aside(j, g):
        chunk_copy(j, g, side_send, sibling).start()

    def await_chunk(j, g, first=0):
        ref = kv.at[j, g, :, first:rows, :]
        pltpu.make_async_copy(ref, ref, kv_recv.at[j, g]).wait()

    def absorb(j, start):
        keys = kv[j, :, 0].reshape(n_seq * tok, HD)
        values = kv[j, :, 1].reshape(n_seq * tok, HD)
        shade = bias[pl.ds(j, 1), :]
        for g in range(n_x):
            at = slice(g * rows, (g + 1) * rows)
            scores = lax.dot_general(
                qbuf[g], keys, (((1,), (1,)), ((), ())), preferred_element_type=jnp.float32
            )
            if not start:
                scores = scores + shade
            largest = jnp.max(scores, axis=-1, keepdims=True)
            if not start:
                largest = jnp.maximum(largest, top[at, 0:1])
            weights = jnp.exp2((scores - largest) * RAISE)
            summed = jnp.dot(weights.astype(jnp.bfloat16), values, preferred_element_type=jnp.float32)
            added = jnp.sum(weights, axis=-1, keepdims=True)
            if not start:
                shrink = jnp.exp2((top[at, 0:1] - largest) * RAISE)
                summed = accum[at, :] * shrink + summed
                added = total[at, 0:1] * shrink + added
            top[at, 0:1] = largest
            total[at, 0:1] = added
            accum[at, :] = summed

    for g in range(n_x):
        await_chunk(span, g, tok if g == 0 else 0)
        pass_on(span, g)

        @pl.when(core == 0)
        def _():
            pass_aside(span, g)

    def take(h):
        @pl.when(chip >= h)
        def _():
            for g in range(n_x):
                await_chunk(span - 2 * h, g)
                pass_on(span - 2 * h, g)
                pass_aside(span - 2 * h, g)

    def from_side(h):
        def run():
            j = sibling - 2 * h
            for g in range(n_x):
                await_chunk(j, g)
            absorb(j, False)

        if h == 0:
            pl.when(core == 1)(run)
        else:
            pl.when(chip >= h)(run)

    take(1)
    q_rest = q_stage.at[1:n_seq]
    pltpu.make_async_copy(q_rest, q_rest, q_recv).wait()
    absorb(span, True)
    from_side(0)
    for h in range(1, n_chip):
        if h + 1 < n_chip:
            take(h + 1)

        @pl.when(chip >= h)
        def _():
            absorb(span - 2 * h, False)

        from_side(h)

    for g in range(n_x):
        at = slice(g * rows, (g + 1) * rows)
        attended = accum[at, :] / total[at, 0:1]
        obuf[at, :] = (attended * gate_row[0:1, :]).astype(jnp.bfloat16)
        if g == 0:
            out_ref[0, :, pl.ds(pl.multiple_of(seq * HD, HD), HD)] = obuf[0:tok, :]

        @pl.loop(1 if g == 0 else 0, n_z)
        def _(r):
            pltpu.make_async_remote_copy(
                src_ref=obuf.at[pl.ds(pl.multiple_of(g * rows + r * tok, tok), tok), :],
                dst_ref=out_ref.at[0, :, pl.ds(pl.multiple_of(seq * HD, HD), HD)],
                send_sem=o_send,
                recv_sem=o_recv,
                device_id={"seq": behind(g, r)},
            ).start()

    def drain(ref, sem):
        pltpu.make_async_copy(ref, ref, sem).wait()

    drain(kv_stage.at[1:n_seq], kv_send)
    drain(q_stage.at[1:n_seq], q_send)
    for h in range(n_chip):

        @pl.when((chip >= h) & (chip < n_chip - 1))
        def _():
            for g in range(n_x):
                chunk_copy(span - 2 * h, g, down_send, span + 2).wait_send()

        @pl.when((chip >= h) & ((core == 0) | (h > 0)))
        def _():
            for g in range(n_x):
                chunk_copy(span - 2 * h, g, side_send, sibling).wait_send()

    drain(obuf.at[tok:, :], o_send)
    drain(out_ref.at[0, :, 0 : (n_seq - 1) * HD], o_recv)


def body(queries, keys, values, timesteps, history, gate_weight):
    n_span, n_seq = lax.axis_size("span"), lax.axis_size("seq")
    n_x = 4 if n_seq == 32 else 2
    n_z = n_seq // n_x
    tok, width = queries.shape[1], queries.shape[2]
    bf16, f32 = jnp.bfloat16, jnp.float32
    rows = n_z * tok
    whole = n_seq * tok
    anywhere = pl.BlockSpec(memory_space=pl.ANY)
    vmem = pl.BlockSpec(memory_space=pltpu.VMEM)
    return pl.pallas_call(
        functools.partial(kernel, n_span, n_x, n_z, tok),
        out_shape=jax.ShapeDtypeStruct(queries.shape, bf16),
        in_specs=[anywhere] * 3 + [pl.BlockSpec(memory_space=pltpu.SMEM), vmem, vmem],
        out_specs=vmem,
        scratch_shapes=[
            pltpu.VMEM((tok, width), bf16),
            pltpu.VMEM((tok, width), bf16),
            pltpu.VMEM((tok, width), bf16),
            pltpu.VMEM((n_seq, 2, tok, HD), bf16),
            pltpu.VMEM((n_seq, tok, HD), bf16),
            pltpu.VMEM((n_span, n_x, 2, rows, HD), bf16),
            pltpu.VMEM((n_x, rows, HD), bf16),
            pltpu.VMEM((whole, HD), bf16),
            pltpu.VMEM((n_span, whole), f32),
            pltpu.VMEM((8, HD), f32),
            pltpu.VMEM((whole, HD), f32),
            pltpu.VMEM((whole, HD), f32),
            pltpu.VMEM((whole, HD), f32),
            pltpu.SemaphoreType.DMA((3,)),
            pltpu.SemaphoreType.DMA((n_span, n_x)),
            pltpu.SemaphoreType.DMA,
            pltpu.SemaphoreType.DMA,
            pltpu.SemaphoreType.DMA,
            pltpu.SemaphoreType.DMA((n_span, n_x)),
            pltpu.SemaphoreType.DMA((n_span, n_x)),
            pltpu.SemaphoreType.DMA,
            pltpu.SemaphoreType.DMA,
        ],
        compiler_params=pltpu.CompilerParams(collective_id=0, has_side_effects=True, vmem_limit_bytes=60 * 2**20),
        name="attention",
    )(queries, keys, values, timesteps, history, gate_weight)


def solution(mesh):
    return jax.shard_map(
        body,
        mesh=mesh,
        in_specs=(
            P(("rep", "span"), "seq", None),
            P(("rep", "span"), "seq", None),
            P(("rep", "span"), "seq", None),
            P(("rep", "span")),
            P(("rep", "span"), None),
            P(None, "seq"),
        ),
        out_specs=P(("rep", "span"), "seq", None),
        check_vma=False,
    )
```

```python
import functools
import math

import jax
import jax.numpy as jnp
from jax import lax
from jax.experimental import pallas as pl
from jax.experimental.pallas import tpu as pltpu
from jax.sharding import PartitionSpec as P

HD = 128
FREQ = 256
RAISE = math.log2(math.e) / math.sqrt(HD)
HIDDEN = -1e30
VLIM = 60
WG = 3
LAG = 1
GN = 4


def places(n_x, n_z, n_g):
    def far(p):
        return (min(p[1], n_z - p[1]), min(p[0], n_x - p[0]))

    every = sorted(((a, b) for a in range(n_x) for b in range(n_z)), key=lambda p: (sum(far(p)), p))
    per = len(every) // n_g
    return every[:per] + sorted(every[per:], key=lambda p: (-far(p)[0], -far(p)[1], p))


def kernel(
    n_span, n_x, n_z, n_g, wrap, tok,
    q_hbm, k_hbm, v_hbm, steps_hbm, history_hbm, gatew_hbm,
    out_ref,
    q_in, k_in, v_in, steps, history, gatew, kv_stage, q_stage, kv, relay, qbuf, obuf, bias, gate_row, top, total, accum,
    in_sem, kv_recv, kv_send, q_recv, q_send, down_send, side_send, wrap_send, relay_recv, relay_send, o_recv, o_send,
):
    n_seq = n_x * n_z
    n_wrap = min(WG, n_g)
    per = n_seq // n_g
    rows = per * tok
    n_chip = n_span // 2
    span, seq, video = lax.axis_index("span"), lax.axis_index("seq"), lax.axis_index("rep")
    chip, core = span // 2, lax.rem(span, 2)
    x, z = seq // n_z, lax.rem(seq, n_z)
    offsets = places(n_x, n_z, n_g)
    x_to = [lax.rem(x + d, n_x) * n_z for d in range(n_x)]
    z_to = [lax.rem(z + d, n_z) for d in range(n_z)]
    ahead = [x_to[a] + z_to[b] for a, b in offsets]
    behind = [x_to[(n_x - a) % n_x] + z_to[(n_z - b) % n_z] for a, b in offsets]
    slots = [(s, s // per, slice(s % per * tok, (s % per + 1) * tok)) for s in range(n_seq)]
    far_first = sorted(
        slots[1:],
        key=lambda s: tuple(-min(d, n - d) for d, n in zip(offsets[s[0]][::-1], (n_z, n_x))),
    )

    fetch = [
        pltpu.make_async_copy(src, dst, in_sem.at[i])
        for i, (src, dst) in enumerate((
            (k_hbm.at[0], k_in), (v_hbm.at[0], v_in), (q_hbm.at[0], q_in),
            (steps_hbm, steps), (history_hbm, history), (gatew_hbm, gatew),
        ))
    ]
    for copy in fetch:
        copy.start()
    barrier = pltpu.get_barrier_semaphore()
    sibling = span + 1 - 2 * core
    last = n_chip - 1
    hop1, hop2 = {"rep": 1 - video, "span": 2 + core}, {"rep": 1 - video, "span": 2 * last + core}

    def greet(to):
        pl.semaphore_signal(barrier, inc=1, device_id=to)

    for s, _, _ in far_first:
        greet({"seq": ahead[s]})
    greet({"span": sibling})
    pl.when(chip > 0)(lambda: greet({"span": span - 2}))
    pl.when(chip < last)(lambda: greet({"span": span + 2}))
    others = n_seq + (chip > 0).astype(jnp.int32) + (chip < last).astype(jnp.int32)
    if wrap:
        pl.when(chip == 0)(lambda: greet(hop1))
        pl.when(chip == 1)(lambda: greet({"rep": 1 - video, "span": core}))
        pl.when(chip == 1)(lambda: greet(hop2))
        pl.when(chip == last)(lambda: greet(hop1))
        others += (chip < 2).astype(jnp.int32) + (chip == 1).astype(jnp.int32) + (chip == last).astype(jnp.int32)

    for copy, inputs, stage in zip(fetch, (k_in, v_in, q_in), (kv_stage.at[:, 0], kv_stage.at[:, 1], q_stage)):
        copy.wait()
        for t in range(n_seq):
            stage[t] = inputs[:, t * HD : (t + 1) * HD]
    kv[span, 0, :, 0:tok, :] = kv_stage[seq]
    qbuf[0:tok, :] = q_stage[seq]
    pl.semaphore_wait(barrier, others)

    for s, g, at in slots[1:]:
        pltpu.make_async_remote_copy(
            src_ref=kv_stage.at[ahead[s]],
            dst_ref=kv.at[span, g, :, at, :],
            send_sem=kv_send,
            recv_sem=kv_recv.at[span, g],
            device_id={"seq": ahead[s]},
        ).start()
    for s, _, _ in far_first:
        pltpu.make_async_remote_copy(
            src_ref=q_stage.at[ahead[s]],
            dst_ref=qbuf.at[s * tok : (s + 1) * tok, :],
            send_sem=q_send,
            recv_sem=q_recv,
            device_id={"seq": ahead[s]},
        ).start()

    for copy in fetch[3:]:
        copy.wait()
    half = FREQ // 2
    k_index = lax.broadcasted_iota(jnp.int32, (8, half), 1).astype(jnp.float32)
    freqs = jnp.exp(-math.log(10000.0) * k_index / half)
    angle = steps[0].astype(jnp.float32) * freqs
    embedding = jnp.concatenate([jnp.cos(angle), jnp.sin(angle)], axis=-1).astype(jnp.bfloat16)
    gate_row[...] = jnp.dot(embedding, gatew[...], preferred_element_type=jnp.float32)

    n_block = n_span * n_seq
    spread = jnp.where(
        lax.broadcasted_iota(jnp.int32, (n_span, n_block), 1) // n_seq
        == lax.broadcasted_iota(jnp.int32, (n_span, n_block), 0),
        history[...],
        0,
    ).astype(jnp.float32).astype(jnp.bfloat16)
    key_slot = lax.broadcasted_iota(jnp.int32, (1, n_seq * tok), 1) // tok
    key_block = jnp.zeros(key_slot.shape, jnp.int32)
    for s in range(n_seq):
        key_block = jnp.where(key_slot == s, behind[s], key_block)
    place = lax.rem(lax.broadcasted_iota(jnp.int32, (n_block, n_seq * tok), 0), n_seq) == key_block
    shown = jnp.dot(
        spread, jnp.where(place, 1.0, 0.0).astype(jnp.bfloat16), preferred_element_type=jnp.float32
    )
    own = lax.broadcasted_iota(jnp.int32, shown.shape, 0) == span
    shade = jnp.where(own | (shown > 0.5), 0.0, HIDDEN)
    for part in range(2):
        bias[part] = shade[:, part * (n_g // 2 * rows) : (part + 1) * (n_g // 2 * rows)]
    top[...] = jnp.full(top.shape, HIDDEN, jnp.float32)
    total[...] = jnp.zeros(total.shape, jnp.float32)
    accum[...] = jnp.zeros(accum.shape, jnp.float32)

    def chunk_copy(j, g, sems, to):
        return pltpu.make_async_remote_copy(
            src_ref=kv.at[j, g],
            dst_ref=kv.at[j, g],
            send_sem=sems.at[j, g],
            recv_sem=kv_recv.at[j, g],
            device_id=to,
        )

    def wrap_copy(g):
        return pltpu.make_async_remote_copy(
            src_ref=kv.at[span, g],
            dst_ref=relay.at[g],
            send_sem=wrap_send.at[g],
            recv_sem=relay_recv.at[g],
            device_id=hop1,
        )

    def relay_copy(g):
        return pltpu.make_async_remote_copy(
            src_ref=relay.at[g],
            dst_ref=kv.at[core, g],
            send_sem=relay_send.at[g],
            recv_sem=kv_recv.at[core, g],
            device_id=hop2,
        )

    def goes_on(h, g):
        if wrap and g < n_wrap:
            return (chip < last) & ((chip < last - 1) | (h < last - 1))
        return chip < last

    def await_chunk(j, g, first=0):
        ref = kv.at[j, g, :, first:rows, :]
        pltpu.make_async_copy(ref, ref, kv_recv.at[j, g]).wait()

    def absorb(j, part):
        mine = pl.ds(part * (n_g // 2), n_g // 2)
        wide = n_g // 2 * rows
        keys = kv[j, mine, 0].reshape(wide, HD)
        values = kv[j, mine, 1].reshape(wide, HD)
        scores = lax.dot_general(
            qbuf[...], keys, (((1,), (1,)), ((), ())), preferred_element_type=jnp.float32
        )
        scores = scores + bias[part, pl.ds(j, 1), :]
        largest = jnp.maximum(jnp.max(scores, axis=-1, keepdims=True), top[...])
        step = min(HD, wide)
        weights = [
            jnp.exp2((scores[:, a : a + step] - largest[:, :step]) * RAISE) for a in range(0, wide, step)
        ]
        added = functools.reduce(jnp.add, weights)
        weights = jnp.concatenate([w.astype(jnp.bfloat16) for w in weights], axis=1)
        summed = jnp.dot(weights, values, preferred_element_type=jnp.float32)
        shrink = jnp.exp2((top[...] - largest) * RAISE)
        total[:, :step] = total[:, :step] * shrink[:, :step] + added
        accum[...] = accum[...] * shrink + summed
        top[...] = largest

    for g in range(n_g):
        if per > 1 or g > 0:
            await_chunk(span, g, tok if g == 0 else 0)
        pl.when(goes_on(0, g))(chunk_copy(span, g, down_send, {"span": span + 2}).start)
        if wrap and g < n_wrap:
            pl.when(chip == 0)(wrap_copy(g).start)
        pl.when(core == 0)(chunk_copy(span, g, side_send, {"span": sibling}).start)

    def take(h, g):
        j = span - 2 * h
        await_chunk(j, g)
        pl.when(goes_on(h, g))(chunk_copy(j, g, down_send, {"span": span + 2}).start)
        chunk_copy(j, g, side_send, {"span": sibling}).start()

    for g in range(n_g + LAG):
        if g < n_g:
            pl.when(chip >= 1)(functools.partial(take, 1, g))
        if wrap and 0 <= g - LAG < n_wrap:

            @pl.when(chip == 1)
            def _():
                here = relay.at[g - LAG]
                pltpu.make_async_copy(here, here, relay_recv.at[g - LAG]).wait()
                relay_copy(g - LAG).start()

    q_rest = q_stage.at[1:n_seq]
    pltpu.make_async_copy(q_rest, q_rest, q_recv).wait()

    @pl.loop(0, chip + 1)
    def _(h):
        @pl.loop(0, 2)
        def _(part):
            @pl.when(h > 1)
            def _():
                for g in range(n_g):
                    pl.when(part == g // (n_g // 2))(functools.partial(take, h, g))

            @pl.loop(0, jnp.where((h > 0) | (core == 1), 2, 1))
            def _(side):
                j = jnp.where(side == 1, sibling, span) - 2 * h

                @pl.when(side == 1)
                def _():
                    for g in range(n_g // 2):
                        await_chunk(j, part * (n_g // 2) + g)

                absorb(j, part)

    for g in list(range(1, n_g)) + [0]:
        at = slice(g * rows, (g + 1) * rows)
        whole = jnp.sum(total[at, : min(HD, n_g // 2 * rows)], axis=-1, keepdims=True)
        obuf[at, :] = (accum[at, :] / whole * gate_row[0:1, :]).astype(jnp.bfloat16)
        for s, _, _ in far_first:
            if s // per == g:
                pltpu.make_async_remote_copy(
                    src_ref=obuf.at[s * tok : (s + 1) * tok, :],
                    dst_ref=out_ref.at[0, :, pl.ds(pl.multiple_of(seq * HD, HD), HD)],
                    send_sem=o_send,
                    recv_sem=o_recv,
                    device_id={"seq": behind[s]},
                ).start()
    out_ref[0, :, pl.ds(pl.multiple_of(seq * HD, HD), HD)] = obuf[0:tok, :]

    def drain(ref, sem):
        pltpu.make_async_copy(ref, ref, sem).wait()

    drain(kv_stage.at[1:n_seq], kv_send)
    drain(q_stage.at[1:n_seq], q_send)
    for h in range(n_chip):

        @pl.when(chip >= h)
        def _():
            for g in range(n_g):
                pl.when(goes_on(h, g))(chunk_copy(span - 2 * h, g, down_send, {"span": span + 2}).wait_send)

        @pl.when((chip >= h) & ((core == 0) | (h > 0)))
        def _():
            for g in range(n_g):
                chunk_copy(span - 2 * h, g, side_send, {"span": sibling}).wait_send()

    if wrap:
        for g in range(n_wrap):
            pl.when(chip == 0)(wrap_copy(g).wait_send)
            pl.when(chip == 1)(relay_copy(g).wait_send)
    drain(obuf.at[tok:, :], o_send)
    drain(out_ref.at[0, :, 0 : (n_seq - 1) * HD], o_recv)


def body(queries, keys, values, timesteps, history, gate_weight):
    n_span, n_seq = lax.axis_size("span"), lax.axis_size("seq")
    n_x = 4 if n_seq == 32 else 2
    n_z = n_seq // n_x
    n_g = GN if n_seq == 32 else 2
    wrap = n_span == 8 and lax.axis_size("rep") == 2
    tok, width = queries.shape[1], queries.shape[2]
    bf16, f32 = jnp.bfloat16, jnp.float32
    rows = n_seq // n_g * tok
    whole = n_seq * tok
    return pl.pallas_call(
        functools.partial(kernel, n_span, n_x, n_z, n_g, wrap, tok),
        out_shape=jax.ShapeDtypeStruct(queries.shape, bf16),
        in_specs=[pl.BlockSpec(memory_space=pltpu.HBM)] * 6,
        out_specs=pl.BlockSpec(memory_space=pltpu.VMEM),
        scratch_shapes=[
            pltpu.VMEM((tok, width), bf16),
            pltpu.VMEM((tok, width), bf16),
            pltpu.VMEM((tok, width), bf16),
            pltpu.SMEM(timesteps.shape, timesteps.dtype),
            pltpu.VMEM(history.shape, history.dtype),
            pltpu.VMEM(gate_weight.shape, bf16),
            pltpu.VMEM((n_seq, 2, tok, HD), bf16),
            pltpu.VMEM((n_seq, tok, HD), bf16),
            pltpu.VMEM((n_span, n_g, 2, rows, HD), bf16),
            pltpu.VMEM((n_g, 2, rows, HD), bf16),
            pltpu.VMEM((whole, HD), bf16),
            pltpu.VMEM((whole, HD), bf16),
            pltpu.VMEM((2, n_span, whole // 2), f32),
            pltpu.VMEM((8, HD), f32),
            pltpu.VMEM((whole, HD), f32),
            pltpu.VMEM((whole, HD), f32),
            pltpu.VMEM((whole, HD), f32),
            pltpu.SemaphoreType.DMA((6,)),
            pltpu.SemaphoreType.DMA((n_span, n_g)),
            pltpu.SemaphoreType.DMA,
            pltpu.SemaphoreType.DMA,
            pltpu.SemaphoreType.DMA,
            pltpu.SemaphoreType.DMA((n_span, n_g)),
            pltpu.SemaphoreType.DMA((n_span, n_g)),
            pltpu.SemaphoreType.DMA((n_g,)),
            pltpu.SemaphoreType.DMA((n_g,)),
            pltpu.SemaphoreType.DMA((n_g,)),
            pltpu.SemaphoreType.DMA,
            pltpu.SemaphoreType.DMA,
        ],
        compiler_params=pltpu.CompilerParams(
            collective_id=0, has_side_effects=True, vmem_limit_bytes=VLIM * 2**20
        ),
        name="attention",
    )(queries, keys, values, timesteps, history, gate_weight)


def solution(mesh):
    return jax.shard_map(
        body,
        mesh=mesh,
        in_specs=(
            P(("rep", "span"), "seq", None),
            P(("rep", "span"), "seq", None),
            P(("rep", "span"), "seq", None),
            P(("rep", "span")),
            P(("rep", "span"), None),
            P(None, "seq"),
        ),
        out_specs=P(("rep", "span"), "seq", None),
        check_vma=False,
    )
```

```python
import functools
import math

import jax
import jax.numpy as jnp
from jax import lax
from jax.experimental import pallas as pl
from jax.experimental.pallas import tpu as pltpu
from jax.sharding import PartitionSpec as P

HD = 128
FREQ = 256
RAISE = math.log2(math.e) / math.sqrt(HD)
HIDDEN = -1e30
VLIM = 60
WG = 3
GN = 4


def places(n_x, n_z, n_g):
    def far(p):
        return (min(p[1], n_z - p[1]), min(p[0], n_x - p[0]))

    every = sorted(((a, b) for a in range(n_x) for b in range(n_z)), key=lambda p: (sum(far(p)), p))
    per = len(every) // n_g
    return every[:per] + sorted(every[per:], key=lambda p: (-far(p)[0], -far(p)[1], p))


def kernel(
    n_span, n_x, n_z, n_g, wrap, tok,
    q_hbm, k_hbm, v_hbm, steps_hbm, history_hbm, gatew_hbm,
    out_ref,
    q_in, k_in, v_in, steps, history, gatew, kv_stage, q_stage, kv, relay, qbuf, obuf, bias, gate_row, top, total, accum,
    in_sem, kv_recv, kv_send, q_recv, q_send, down_send, side_send, wrap_send, relay_recv, relay_send, o_recv, o_send,
):
    n_seq = n_x * n_z
    n_wrap = min(WG, n_g) if wrap else 0
    per = n_seq // n_g
    rows = per * tok
    n_chip = n_span // 2
    span, seq, video = lax.axis_index("span"), lax.axis_index("seq"), lax.axis_index("rep")
    chip, core = span // 2, lax.rem(span, 2)
    x, z = seq // n_z, lax.rem(seq, n_z)
    offsets = places(n_x, n_z, n_g)
    x_to = [lax.rem(x + d, n_x) * n_z for d in range(n_x)]
    z_to = [lax.rem(z + d, n_z) for d in range(n_z)]
    ahead = [x_to[a] + z_to[b] for a, b in offsets]
    behind = [x_to[(n_x - a) % n_x] + z_to[(n_z - b) % n_z] for a, b in offsets]
    slots = [(s, s // per, slice(s % per * tok, (s % per + 1) * tok)) for s in range(n_seq)]
    far_first = sorted(
        slots[1:],
        key=lambda s: tuple(-min(d, n - d) for d, n in zip(offsets[s[0]][::-1], (n_z, n_x))),
    )

    fetch = [
        pltpu.make_async_copy(src, dst, in_sem.at[i])
        for i, (src, dst) in enumerate((
            (k_hbm.at[0], k_in), (v_hbm.at[0], v_in), (q_hbm.at[0], q_in),
            (steps_hbm, steps), (history_hbm, history), (gatew_hbm, gatew),
        ))
    ]
    for copy in fetch:
        copy.start()
    barrier = pltpu.get_barrier_semaphore()
    sibling = span + 1 - 2 * core
    last = n_chip - 1
    hop1, hop2 = {"rep": 1 - video, "span": 2 + core}, {"rep": 1 - video, "span": 2 * last + core}

    def greet(to):
        pl.semaphore_signal(barrier, inc=1, device_id=to)

    for s, _, _ in far_first:
        greet({"seq": ahead[s]})
    greet({"span": sibling})
    pl.when(chip > 0)(lambda: greet({"span": span - 2}))
    pl.when(chip < last)(lambda: greet({"span": span + 2}))
    others = n_seq + (chip > 0).astype(jnp.int32) + (chip < last).astype(jnp.int32)
    if wrap:
        pl.when(chip == 0)(lambda: greet({"span": span + 2 * last}))
        pl.when(chip == last)(lambda: greet({"span": core}))
        pl.when(chip == 0)(lambda: greet(hop1))
        pl.when(chip == 1)(lambda: greet({"rep": 1 - video, "span": core}))
        pl.when(chip == 1)(lambda: greet(hop2))
        pl.when(chip == last)(lambda: greet(hop1))
        others += 2 * (1 - ((chip > 1) & (chip < last)).astype(jnp.int32))

    for copy, inputs, stage in zip(fetch, (k_in, v_in, q_in), (kv_stage.at[:, 0], kv_stage.at[:, 1], q_stage)):
        copy.wait()
        for t in range(n_seq):
            stage[t] = inputs[:, t * HD : (t + 1) * HD]
    kv[span * n_g, :, 0:tok, :] = kv_stage[seq]
    qbuf[0:tok, :] = q_stage[seq]
    pl.semaphore_wait(barrier, others)

    for s, g, at in slots[1:]:
        pltpu.make_async_remote_copy(
            src_ref=kv_stage.at[ahead[s]],
            dst_ref=kv.at[span * n_g + g, :, at, :],
            send_sem=kv_send,
            recv_sem=kv_recv.at[span * n_g + g],
            device_id={"seq": ahead[s]},
        ).start()
    for s, _, _ in far_first:
        pltpu.make_async_remote_copy(
            src_ref=q_stage.at[ahead[s]],
            dst_ref=qbuf.at[s * tok : (s + 1) * tok, :],
            send_sem=q_send,
            recv_sem=q_recv,
            device_id={"seq": ahead[s]},
        ).start()

    for copy in fetch[3:]:
        copy.wait()
    n_freq = FREQ // 2
    k_index = lax.broadcasted_iota(jnp.int32, (8, n_freq), 1).astype(jnp.float32)
    freqs = jnp.exp(-math.log(10000.0) * k_index / n_freq)
    angle = steps[0].astype(jnp.float32) * freqs
    embedding = jnp.concatenate([jnp.cos(angle), jnp.sin(angle)], axis=-1).astype(jnp.bfloat16)
    gate_row[...] = jnp.dot(embedding, gatew[...], preferred_element_type=jnp.float32)

    n_block = n_span * n_seq
    spread = jnp.where(
        lax.broadcasted_iota(jnp.int32, (n_span, n_block), 1) // n_seq
        == lax.broadcasted_iota(jnp.int32, (n_span, n_block), 0),
        history[...],
        0,
    ).astype(jnp.float32).astype(jnp.bfloat16)
    key_slot = lax.broadcasted_iota(jnp.int32, (1, n_seq * tok), 1) // tok
    key_block = jnp.zeros(key_slot.shape, jnp.int32)
    for s in range(n_seq):
        key_block = jnp.where(key_slot == s, behind[s], key_block)
    place = lax.rem(lax.broadcasted_iota(jnp.int32, (n_block, n_seq * tok), 0), n_seq) == key_block
    shown = jnp.dot(
        spread, jnp.where(place, 1.0, 0.0).astype(jnp.bfloat16), preferred_element_type=jnp.float32
    )
    own = lax.broadcasted_iota(jnp.int32, shown.shape, 0) == span
    shade = jnp.where(own | (shown > 0.5), 0.0, HIDDEN)
    for part in range(2):
        bias[part] = shade[:, part * (n_g // 2 * rows) : (part + 1) * (n_g // 2 * rows)]
    top[...] = jnp.full(top.shape, HIDDEN, jnp.float32)
    total[...] = jnp.zeros(total.shape, jnp.float32)
    accum[...] = jnp.zeros(accum.shape, jnp.float32)

    def chunk_copy(j, g, sems, to):
        return pltpu.make_async_remote_copy(
            src_ref=kv.at[j * n_g + g],
            dst_ref=kv.at[j * n_g + g],
            send_sem=sems,
            recv_sem=kv_recv.at[j * n_g + g],
            device_id=to,
        )

    def wrap_copy(g):
        return pltpu.make_async_remote_copy(
            src_ref=kv.at[span * n_g + g],
            dst_ref=relay.at[g],
            send_sem=wrap_send,
            recv_sem=relay_recv.at[g],
            device_id=hop1,
        )

    def relay_copy(g):
        return pltpu.make_async_remote_copy(
            src_ref=relay.at[g],
            dst_ref=kv.at[core * n_g + g],
            send_sem=relay_send,
            recv_sem=kv_recv.at[core * n_g + g],
            device_id=hop2,
        )

    def goes_on(h):
        if wrap and h == last - 1:
            return chip < 0
        return chip < last

    def await_chunk(j, g, first=0):
        ref = kv.at[j * n_g + g, :, first:rows, :]
        pltpu.make_async_copy(ref, ref, kv_recv.at[j * n_g + g]).wait()

    half = n_g // 2

    def absorb(*pieces):
        wide = half * rows
        keys, values, shade = [], [], []
        for j, part in pieces:
            mine = pl.ds(j * n_g + part * half, half)
            keys.append(kv[mine, 0].reshape(wide, HD))
            values.append(kv[mine, 1].reshape(wide, HD))
            shade.append(bias[part, pl.ds(j, 1), :])
        scores = lax.dot_general(
            qbuf[...], jnp.concatenate(keys), (((1,), (1,)), ((), ())), preferred_element_type=jnp.float32
        )
        scores = scores + jnp.concatenate(shade, axis=1)
        largest = jnp.maximum(jnp.max(scores, axis=-1, keepdims=True), top[...])
        step = min(HD, 2 * wide)
        weights = [
            jnp.exp2((scores[:, a : a + step] - largest[:, :step]) * RAISE) for a in range(0, 2 * wide, step)
        ]
        added = functools.reduce(jnp.add, weights)
        weights = jnp.concatenate([w.astype(jnp.bfloat16) for w in weights], axis=1)
        summed = jnp.dot(weights, jnp.concatenate(values), preferred_element_type=jnp.float32)
        shrink = jnp.exp2((top[...] - largest) * RAISE)
        total[:, :step] = total[:, :step] * shrink[:, :step] + added
        accum[...] = accum[...] * shrink + summed
        top[...] = largest

    for g in range(n_g):
        if per > 1 or g > 0:
            await_chunk(span, g, tok if g == 0 else 0)
        pl.when(goes_on(0))(chunk_copy(span, g, down_send, {"span": span + 2}).start)
        if wrap:
            far = wrap_copy(g) if g < n_wrap else chunk_copy(span, g, down_send, {"span": span + 2 * last})
            pl.when(chip == 0)(far.start)
        pl.when(core == 0)(chunk_copy(span, g, side_send, {"span": sibling}).start)

    def take(h, g):
        j = span - 2 * h
        await_chunk(j, g)
        pl.when(goes_on(h))(chunk_copy(j, g, down_send, {"span": span + 2}).start)
        chunk_copy(j, g, side_send, {"span": sibling}).start()

    def halves(part):
        return range(part * n_g // 2, (part + 1) * n_g // 2)

    def order(c):
        if wrap and c == last and c == 3:
            return [(1, 0), (1, 1), (2, 0), (3, 0), (2, 1), (3, 1)]
        return [(h, part) for h in range(1, c + 1) for part in range(2)]

    def passes(c):
        halves_in = order(c)
        if c == 0:
            return {}
        if wrap and c == 1:
            return {-1: [(1, 0)], 0: [0, (1, 1), 1], 1: [2, 3]}
        if c < last:
            ahead_of = {-1: [(1, 0), (1, 1)]}
            rest = halves_in[2:]
        else:
            ahead_of = {-1: [(1, 0)]}
            rest = halves_in[1:]
        for n, one in enumerate(rest):
            ahead_of[n] = [one]
        return ahead_of

    def pass_through(what):
        for one in what:
            if isinstance(one, tuple):
                for g in halves(one[1]):
                    take(one[0], g)
            elif one < n_wrap:
                here = relay.at[one]
                pltpu.make_async_copy(here, here, relay_recv.at[one]).wait()
                relay_copy(one).start()

    for c in range(n_chip):
        if passes(c).get(-1):
            pl.when(chip == c)(functools.partial(pass_through, passes(c)[-1]))
    q_rest = q_stage.at[1:n_seq]
    pltpu.make_async_copy(q_rest, q_rest, q_recv).wait()

    @pl.loop(0, 2 * chip + core + 1)
    def _(i):
        k = i - (1 + core)
        here = k < 0
        h, part = (k + 2) // 2, lax.rem(k + 2, 2)
        if order(last) != [(m // 2 + 1, m % 2) for m in range(2 * last)]:
            for m, (hop, which) in enumerate(order(last)):
                h = jnp.where((chip == last) & (k == m), hop, h)
                part = jnp.where((chip == last) & (k == m), which, part)
        up, side = span - 2 * h, sibling - 2 * h
        for c in range(n_chip):
            for when, what in passes(c).items():
                if when >= 0:
                    pl.when((chip == c) & (k == when))(functools.partial(pass_through, what))

        @pl.when(jnp.logical_not(here))
        def _():
            for g in range(half):
                await_chunk(side, part * half + g)

        @pl.when(here & (i == 1))
        def _():
            for g in range(n_g):
                await_chunk(sibling, g)

        only = jnp.where(i == 1, sibling, span)
        absorb(
            (jnp.where(here, only, up), jnp.where(here, 0, part)),
            (jnp.where(here, only, side), jnp.where(here, 1, part)),
        )

    for g in list(range(1, n_g)) + [0]:
        at = slice(g * rows, (g + 1) * rows)
        whole = jnp.sum(total[at, : min(HD, n_g * rows)], axis=-1, keepdims=True)
        obuf[at, :] = (accum[at, :] / whole * gate_row[0:1, :]).astype(jnp.bfloat16)
        for s, _, _ in far_first:
            if s // per == g:
                pltpu.make_async_remote_copy(
                    src_ref=obuf.at[s * tok : (s + 1) * tok, :],
                    dst_ref=out_ref.at[0, :, pl.ds(pl.multiple_of(seq * HD, HD), HD)],
                    send_sem=o_send,
                    recv_sem=o_recv,
                    device_id={"seq": behind[s]},
                ).start()
    mine = pltpu.make_async_copy(
        obuf.at[0:tok, :], out_ref.at[0, :, pl.ds(pl.multiple_of(seq * HD, HD), HD)], in_sem.at[0]
    )
    mine.start()
    mine.wait()

    def drain(ref, sem):
        pltpu.make_async_copy(ref, ref, sem).wait()

    drain(kv_stage.at[1:n_seq], kv_send)
    drain(q_stage.at[1:n_seq], q_send)
    for c in range(n_chip):
        passed = [h for h in range(c + 1) if not (wrap and h == last - 1)] if c < last else []
        n_down = len(passed) * n_g + (n_g - n_wrap if wrap and c == 0 else 0)
        if n_down:
            pl.when(chip == c)(functools.partial(drain, kv.at[0:n_down], down_send))
        pl.when((chip == c) & (core == 0))(functools.partial(drain, kv.at[0 : (c + 1) * n_g], side_send))
        if c > 0:
            pl.when((chip == c) & (core == 1))(functools.partial(drain, kv.at[0 : c * n_g], side_send))
    if n_wrap:
        pl.when(chip == 0)(functools.partial(drain, relay.at[0:n_wrap], wrap_send))
        pl.when(chip == 1)(functools.partial(drain, relay.at[0:n_wrap], relay_send))
    drain(obuf.at[tok:, :], o_send)
    drain(out_ref.at[0, :, 0 : (n_seq - 1) * HD], o_recv)


def body(queries, keys, values, timesteps, history, gate_weight):
    n_span, n_seq = lax.axis_size("span"), lax.axis_size("seq")
    n_x = 4 if n_seq == 32 else 2
    n_z = n_seq // n_x
    n_g = GN if n_seq == 32 else 2
    wrap = n_span == 8 and lax.axis_size("rep") == 2
    tok, width = queries.shape[1], queries.shape[2]
    bf16, f32 = jnp.bfloat16, jnp.float32
    rows = n_seq // n_g * tok
    whole = n_seq * tok
    return pl.pallas_call(
        functools.partial(kernel, n_span, n_x, n_z, n_g, wrap, tok),
        out_shape=pltpu.VMEM(queries.shape, bf16),
        in_specs=[pl.BlockSpec(memory_space=pltpu.HBM)] * 6,
        out_specs=pl.BlockSpec(memory_space=pltpu.VMEM),
        scratch_shapes=[
            pltpu.VMEM((tok, width), bf16),
            pltpu.VMEM((tok, width), bf16),
            pltpu.VMEM((tok, width), bf16),
            pltpu.SMEM(timesteps.shape, timesteps.dtype),
            pltpu.VMEM(history.shape, history.dtype),
            pltpu.VMEM(gate_weight.shape, bf16),
            pltpu.VMEM((n_seq, 2, tok, HD), bf16),
            pltpu.VMEM((n_seq, tok, HD), bf16),
            pltpu.VMEM((n_span * n_g, 2, rows, HD), bf16),
            pltpu.VMEM((n_g, 2, rows, HD), bf16),
            pltpu.VMEM((whole, HD), bf16),
            pltpu.VMEM((whole, HD), bf16),
            pltpu.VMEM((2, n_span, whole // 2), f32),
            pltpu.VMEM((8, HD), f32),
            pltpu.VMEM((whole, HD), f32),
            pltpu.VMEM((whole, HD), f32),
            pltpu.VMEM((whole, HD), f32),
            pltpu.SemaphoreType.DMA((6,)),
            pltpu.SemaphoreType.DMA((n_span * n_g,)),
            pltpu.SemaphoreType.DMA,
            pltpu.SemaphoreType.DMA,
            pltpu.SemaphoreType.DMA,
            pltpu.SemaphoreType.DMA,
            pltpu.SemaphoreType.DMA,
            pltpu.SemaphoreType.DMA,
            pltpu.SemaphoreType.DMA((n_g,)),
            pltpu.SemaphoreType.DMA,
            pltpu.SemaphoreType.DMA,
            pltpu.SemaphoreType.DMA,
        ],
        compiler_params=pltpu.CompilerParams(
            collective_id=0, has_side_effects=True, vmem_limit_bytes=VLIM * 2**20
        ),
        name="attention",
    )(queries, keys, values, timesteps, history, gate_weight)


def solution(mesh):
    return jax.shard_map(
        body,
        mesh=mesh,
        in_specs=(
            P(("rep", "span"), "seq", None),
            P(("rep", "span"), "seq", None),
            P(("rep", "span"), "seq", None),
            P(("rep", "span")),
            P(("rep", "span"), None),
            P(None, "seq"),
        ),
        out_specs=P(("rep", "span"), "seq", None),
        check_vma=False,
    )
```

```python
import functools
import math

import jax
import jax.numpy as jnp
from jax import lax
from jax.experimental import pallas as pl
from jax.experimental.pallas import tpu as pltpu
from jax.sharding import PartitionSpec as P

HD = 128
FREQ = 256
RAISE = math.log2(math.e) / math.sqrt(HD)
HIDDEN = -1e30
VLIM = 60
WG = 3
GN = 4


def places(n_x, n_z, n_g):
    def far(p):
        return (min(p[1], n_z - p[1]), min(p[0], n_x - p[0]))

    def far_first(p):
        return (-far(p)[0], -far(p)[1], p)

    every = sorted(((a, b) for a in range(n_x) for b in range(n_z)), key=lambda p: (far(p), p))
    per = len(every) // n_g
    rest = sorted(every[per:], key=lambda p: (sum(far(p)), p))
    return every[:per] + sorted(rest[:per], key=far_first) + sorted(rest[per:], key=far_first)


def kernel(
    n_span, n_x, n_z, n_g, wrap, tok,
    q_hbm, k_hbm, v_hbm, steps_hbm, history_hbm, gatew_hbm,
    out_ref,
    q_in, k_in, v_in, steps, history, gatew, kv_stage, q_stage, kv, relay, qbuf, obuf, bias, gate_row, top, total, accum,
    in_sem, kv_recv, kv_send, direct_send, q_recv, q_send, down_send, side_send, wrap_send, relay_recv, relay_send, o_recv, o_send,
):
    n_seq = n_x * n_z
    n_wrap = min(WG, n_g) if wrap else 0
    n_direct = 1
    per = n_seq // n_g
    rows = per * tok
    n_chip = n_span // 2
    span, seq, video = lax.axis_index("span"), lax.axis_index("seq"), lax.axis_index("rep")
    chip, core = span // 2, lax.rem(span, 2)
    x, z = seq // n_z, lax.rem(seq, n_z)
    offsets = places(n_x, n_z, n_g)
    x_to = [lax.rem(x + d, n_x) * n_z for d in range(n_x)]
    z_to = [lax.rem(z + d, n_z) for d in range(n_z)]
    ahead = [x_to[a] + z_to[b] for a, b in offsets]
    behind = [x_to[(n_x - a) % n_x] + z_to[(n_z - b) % n_z] for a, b in offsets]
    slots = [(s, s // per, slice(s % per * tok, (s % per + 1) * tok)) for s in range(n_seq)]
    far_first = sorted(
        slots[1:],
        key=lambda s: tuple(-min(d, n - d) for d, n in zip(offsets[s[0]][::-1], (n_z, n_x))),
    )

    fetch = [
        pltpu.make_async_copy(src, dst, in_sem.at[i])
        for i, (src, dst) in enumerate((
            (k_hbm.at[0], k_in), (v_hbm.at[0], v_in), (q_hbm.at[0], q_in),
            (steps_hbm, steps), (history_hbm, history), (gatew_hbm, gatew),
        ))
    ]
    for copy in fetch:
        copy.start()
    barrier = pltpu.get_barrier_semaphore()
    sibling = span + 1 - 2 * core
    last = n_chip - 1
    hop1, hop2 = {"rep": 1 - video, "span": 2 + core}, {"rep": 1 - video, "span": 2 * last + core}

    def greet(to):
        pl.semaphore_signal(barrier, inc=1, device_id=to)

    for s, _, _ in far_first:
        greet({"seq": ahead[s]})
    greet({"span": sibling})
    pl.when(chip > 0)(lambda: greet({"span": span - 2}))
    pl.when(chip < last)(lambda: greet({"span": span + 2}))
    near = slots[:per]

    def greet_near(to):
        for s, _, _ in near[1:]:
            greet({**to, "seq": behind[s]})

    others = n_seq
    pl.when(chip > 0)(lambda: greet_near({"span": span - 2}))
    others += (per - 1) * (chip < last).astype(jnp.int32)
    others += (chip > 0).astype(jnp.int32) + (chip < last).astype(jnp.int32)
    if wrap:
        pl.when(chip == 0)(lambda: greet({"span": span + 2 * last}))
        pl.when(chip == last)(lambda: greet({"span": core}))
        pl.when(chip == 0)(lambda: greet(hop1))
        pl.when(chip == 1)(lambda: greet({"rep": 1 - video, "span": core}))
        pl.when(chip == 1)(lambda: greet(hop2))
        pl.when(chip == last)(lambda: greet(hop1))
        others += 2 * (1 - ((chip > 1) & (chip < last)).astype(jnp.int32))

    for copy, inputs, stage in zip(fetch, (k_in, v_in, q_in), (kv_stage.at[:, 0], kv_stage.at[:, 1], q_stage)):
        copy.wait()
        for t in range(n_seq):
            stage[t] = inputs[:, t * HD : (t + 1) * HD]
    kv[span * n_g, :, 0:tok, :] = kv_stage[seq]
    qbuf[0:tok, :] = q_stage[seq]
    pl.semaphore_wait(barrier, others)

    def send_near():
        for s, g, at in near:
            pltpu.make_async_remote_copy(
                src_ref=kv_stage.at[ahead[s]],
                dst_ref=kv.at[span * n_g + g, :, at, :],
                send_sem=direct_send,
                recv_sem=kv_recv.at[span * n_g + g],
                device_id={"span": span + 2, "seq": ahead[s]},
            ).start()

    pl.when(chip < last)(send_near)
    for s, g, at in slots[1:]:
        pltpu.make_async_remote_copy(
            src_ref=kv_stage.at[ahead[s]],
            dst_ref=kv.at[span * n_g + g, :, at, :],
            send_sem=kv_send,
            recv_sem=kv_recv.at[span * n_g + g],
            device_id={"seq": ahead[s]},
        ).start()
    for s, _, _ in far_first:
        pltpu.make_async_remote_copy(
            src_ref=q_stage.at[ahead[s]],
            dst_ref=qbuf.at[s * tok : (s + 1) * tok, :],
            send_sem=q_send,
            recv_sem=q_recv,
            device_id={"seq": ahead[s]},
        ).start()

    for copy in fetch[3:]:
        copy.wait()
    n_freq = FREQ // 2
    k_index = lax.broadcasted_iota(jnp.int32, (8, n_freq), 1).astype(jnp.float32)
    freqs = jnp.exp(-math.log(10000.0) * k_index / n_freq)
    angle = steps[...].astype(jnp.float32) * freqs
    embedding = jnp.concatenate([jnp.cos(angle), jnp.sin(angle)], axis=-1).astype(jnp.bfloat16)
    gate_row[...] = jnp.dot(embedding, gatew[...], preferred_element_type=jnp.float32)

    n_block = n_span * n_seq
    spread = jnp.where(
        lax.broadcasted_iota(jnp.int32, (n_span, n_block), 1) // n_seq
        == lax.broadcasted_iota(jnp.int32, (n_span, n_block), 0),
        history[...],
        0,
    ).astype(jnp.float32).astype(jnp.bfloat16)
    key_slot = lax.broadcasted_iota(jnp.int32, (1, n_seq * tok), 1) // tok
    key_block = jnp.zeros(key_slot.shape, jnp.int32)
    for s in range(n_seq):
        key_block = jnp.where(key_slot == s, behind[s], key_block)
    place = lax.rem(lax.broadcasted_iota(jnp.int32, (n_block, n_seq * tok), 0), n_seq) == key_block
    shown = jnp.dot(
        spread, jnp.where(place, 1.0, 0.0).astype(jnp.bfloat16), preferred_element_type=jnp.float32
    )
    own = lax.broadcasted_iota(jnp.int32, shown.shape, 0) == span
    shade = jnp.where(own | (shown > 0.5), 0.0, HIDDEN)
    for part in range(2):
        bias[part] = shade[:, part * (n_g // 2 * rows) : (part + 1) * (n_g // 2 * rows)]
    top[...] = jnp.full(top.shape, HIDDEN, jnp.float32)
    total[...] = jnp.zeros(total.shape, jnp.float32)
    accum[...] = jnp.zeros(accum.shape, jnp.float32)

    def chunk_copy(j, g, sems, to):
        return pltpu.make_async_remote_copy(
            src_ref=kv.at[j * n_g + g],
            dst_ref=kv.at[j * n_g + g],
            send_sem=sems,
            recv_sem=kv_recv.at[j * n_g + g],
            device_id=to,
        )

    def wrap_copy(g):
        return pltpu.make_async_remote_copy(
            src_ref=kv.at[span * n_g + g],
            dst_ref=relay.at[g],
            send_sem=wrap_send,
            recv_sem=relay_recv.at[g],
            device_id=hop1,
        )

    def relay_copy(g):
        return pltpu.make_async_remote_copy(
            src_ref=relay.at[g],
            dst_ref=kv.at[core * n_g + g],
            send_sem=relay_send,
            recv_sem=kv_recv.at[core * n_g + g],
            device_id=hop2,
        )

    def goes_on(h):
        if wrap and h == last - 1:
            return chip < 0
        return chip < last

    def await_chunk(j, g, first=0):
        ref = kv.at[j * n_g + g, :, first:rows, :]
        pltpu.make_async_copy(ref, ref, kv_recv.at[j * n_g + g]).wait()

    half = n_g // 2

    def absorb(*pieces):
        wide = half * rows
        keys, values, shade = [], [], []
        for j, part in pieces:
            mine = pl.ds(j * n_g + part * half, half)
            keys.append(kv[mine, 0].reshape(wide, HD))
            values.append(kv[mine, 1].reshape(wide, HD))
            shade.append(bias[part, pl.ds(j, 1), :])
        scores = lax.dot_general(
            qbuf[...], jnp.concatenate(keys), (((1,), (1,)), ((), ())), preferred_element_type=jnp.float32
        )
        scores = scores + jnp.concatenate(shade, axis=1)
        largest = jnp.maximum(jnp.max(scores, axis=-1, keepdims=True), top[...])
        step = min(HD, 2 * wide)
        weights = [
            jnp.exp2((scores[:, a : a + step] - largest[:, :step]) * RAISE) for a in range(0, 2 * wide, step)
        ]
        added = functools.reduce(jnp.add, weights)
        weights = jnp.concatenate([w.astype(jnp.bfloat16) for w in weights], axis=1)
        summed = jnp.dot(weights, jnp.concatenate(values), preferred_element_type=jnp.float32)
        shrink = jnp.exp2((top[...] - largest) * RAISE)
        total[:, :step] = total[:, :step] * shrink[:, :step] + added
        accum[...] = accum[...] * shrink + summed
        top[...] = largest

    def take(h, g):
        j = span - 2 * h
        await_chunk(j, g)
        pl.when(goes_on(h))(chunk_copy(j, g, down_send, {"span": span + 2}).start)
        chunk_copy(j, g, side_send, {"span": sibling}).start()

    pl.when(chip > 0)(functools.partial(take, 1, 0))
    for g in range(n_g):
        if per > 1 or g > 0:
            await_chunk(span, g, tok if g == 0 else 0)
        if g >= n_direct:
            pl.when(goes_on(0))(chunk_copy(span, g, down_send, {"span": span + 2}).start)
        if g < n_wrap:
            pl.when(chip == 0)(wrap_copy(g).start)
        pl.when(core == 0)(chunk_copy(span, g, side_send, {"span": sibling}).start)

    def halves(part):
        return range(part * half, (part + 1) * half)

    def do(op, *what):
        if op == "take":
            for g in halves(what[1]):
                if what[0] > 1 or g >= n_direct:
                    take(what[0], g)
        elif op == "side":
            for g in halves(what[1]):
                await_chunk(sibling - 2 * what[0], g)
        elif op == "relay":
            if what[0] < n_wrap:
                here = relay.at[what[0]]
                pltpu.make_async_copy(here, here, relay_recv.at[what[0]]).wait()
                relay_copy(what[0]).start()
        elif op == "far":
            for g in range(n_wrap, n_g) if wrap else []:
                chunk_copy(span, g, down_send, {"span": span + 2 * last}).start()
        elif op == "queries":
            rest = q_stage.at[1:n_seq]
            pltpu.make_async_copy(rest, rest, q_recv).wait()

    def plan(c, k):
        def take_both(h):
            return [("take", h, 0), ("take", h, 1)]

        def side_both(h):
            return [("side", h, 0), ("side", h, 1)]

        def whole(d):
            return [((d, 0), (d, 1))]

        def up(h):
            return whole(-2 * h)

        def side(h):
            return side_both(h) + whole(1 - 2 * k - 2 * h)

        def both_up(part):
            return [((-2 * (last - 1), part), (-2 * last, part))]

        def both_side(part):
            d = 1 - 2 * k
            return [("side", last - 1, part), ("side", last, part), ((d - 2 * (last - 1), part), (d - 2 * last, part))]

        start = [("queries",)] + whole(0)
        relays = [[("relay", g)] for g in range(n_g)] + [[]] * 4
        if c == 0:
            return start[:1] + [("far",)] + start[1:] + (side(0) if k == 1 else [])
        if c == 1 and k == 0:
            return ([("take", 1, 0)] + start + relays[0] + [("take", 1, 1)] + relays[1] + side(1) + relays[2] + relays[3]
                    + up(1))
        if c == 1:
            return (take_both(1) + start + relays[0] + up(1) + relays[1] + side(0) + relays[2] + relays[3] + side(1))
        if c == 2 and k == 0:
            return ([("take", 1, 0)] + start + side(1) + [("take", 1, 1)] + up(1) + side(2) + take_both(2) + up(2))
        if c == 2:
            return take_both(1) + start + up(1) + side(0) + take_both(2) + up(2) + side(1) + side(2)
        if k == 0:
            return ([("take", 1, 0)] + start + side(1) + [("take", 1, 1)] + up(1)
                    + [("take", 2, 0)] + side(2) + [("take", 3, 0)] + both_up(0)
                    + [("take", 2, 1), ("take", 3, 1)] + side(3)
                    + both_up(1))
        return (take_both(1) + start + up(1) + side(0) + take_both(2) + up(2) + side(1) + take_both(3) + up(3)
                + both_side(0) + both_side(1))

    def run(c, k):
        steps, waits = [], []
        for one in plan(c, k):
            if isinstance(one[0], str):
                waits.append(one)
            else:
                steps.append((waits, one))
                waits = []

        @pl.loop(0, len(steps))
        def _(i):
            pieces = [[jnp.int32(0), jnp.int32(0)], [jnp.int32(0), jnp.int32(0)]]
            for n, (waits, pair) in enumerate(steps):

                @pl.when(i == n)
                def _():
                    for one in waits:
                        do(*one)

                for piece, (distance, part) in zip(pieces, pair):
                    piece[0] = jnp.where(i == n, distance, piece[0])
                    piece[1] = jnp.where(i == n, part, piece[1])
            absorb(*((span + distance, part) for distance, part in pieces))

    for c in range(n_chip):
        for k in range(2):
            pl.when((chip == c) & (core == k))(functools.partial(run, c, k))

    for g in reversed(range(n_g)):
        at = slice(g * rows, (g + 1) * rows)
        whole = jnp.sum(total[at, : min(HD, n_g * rows)], axis=-1, keepdims=True)
        obuf[at, :] = (accum[at, :] * (1.0 / whole) * gate_row[0:1, :]).astype(jnp.bfloat16)
        for s, _, _ in far_first:
            if s // per == g:
                pltpu.make_async_remote_copy(
                    src_ref=obuf.at[s * tok : (s + 1) * tok, :],
                    dst_ref=out_ref.at[0, :, pl.ds(pl.multiple_of(seq * HD, HD), HD)],
                    send_sem=o_send,
                    recv_sem=o_recv,
                    device_id={"seq": behind[s]},
                ).start()
    mine = pltpu.make_async_copy(
        obuf.at[0:tok, :], out_ref.at[0, :, pl.ds(pl.multiple_of(seq * HD, HD), HD)], in_sem.at[0]
    )
    mine.start()
    mine.wait()

    def drain(ref, sem):
        pltpu.make_async_copy(ref, ref, sem).wait()

    drain(kv_stage.at[1:n_seq], kv_send)
    drain(q_stage.at[1:n_seq], q_send)
    pl.when(chip < last)(functools.partial(drain, kv_stage.at[0:per], direct_send))
    for c in range(n_chip):
        passed = [h for h in range(c + 1) if not (wrap and h == last - 1)] if c < last else []
        n_down = len(passed) * n_g + (n_g - n_wrap if wrap and c == 0 else 0) - (n_direct if c < last else 0)
        if n_down:
            pl.when(chip == c)(functools.partial(drain, kv.at[0:n_down], down_send))
        pl.when((chip == c) & (core == 0))(functools.partial(drain, kv.at[0 : (c + 1) * n_g], side_send))
        if c > 0:
            pl.when((chip == c) & (core == 1))(functools.partial(drain, kv.at[0 : c * n_g], side_send))
    if n_wrap:
        pl.when(chip == 0)(functools.partial(drain, relay.at[0:n_wrap], wrap_send))
        pl.when(chip == 1)(functools.partial(drain, relay.at[0:n_wrap], relay_send))
    drain(obuf.at[tok:, :], o_send)
    drain(out_ref.at[0, :, 0 : (n_seq - 1) * HD], o_recv)


def body(queries, keys, values, timesteps, history, gate_weight):
    n_span, n_seq = lax.axis_size("span"), lax.axis_size("seq")
    n_x = 4 if n_seq == 32 else 2
    n_z = n_seq // n_x
    n_g = GN if n_seq == 32 else 2
    wrap = n_span == 8 and lax.axis_size("rep") == 2
    tok, width = queries.shape[1], queries.shape[2]
    bf16, f32 = jnp.bfloat16, jnp.float32
    rows = n_seq // n_g * tok
    whole = n_seq * tok
    return pl.pallas_call(
        functools.partial(kernel, n_span, n_x, n_z, n_g, wrap, tok),
        out_shape=pltpu.VMEM(queries.shape, bf16),
        in_specs=[pl.BlockSpec(memory_space=pltpu.HBM)] * 6,
        out_specs=pl.BlockSpec(memory_space=pltpu.VMEM),
        scratch_shapes=[
            pltpu.VMEM((tok, width), bf16),
            pltpu.VMEM((tok, width), bf16),
            pltpu.VMEM((tok, width), bf16),
            pltpu.VMEM((1, 1), timesteps.dtype),
            pltpu.VMEM(history.shape, history.dtype),
            pltpu.VMEM(gate_weight.shape, bf16),
            pltpu.VMEM((n_seq, 2, tok, HD), bf16),
            pltpu.VMEM((n_seq, tok, HD), bf16),
            pltpu.VMEM((n_span * n_g, 2, rows, HD), bf16),
            pltpu.VMEM((n_g, 2, rows, HD), bf16),
            pltpu.VMEM((whole, HD), bf16),
            pltpu.VMEM((whole, HD), bf16),
            pltpu.VMEM((2, n_span, whole // 2), f32),
            pltpu.VMEM((8, HD), f32),
            pltpu.VMEM((whole, HD), f32),
            pltpu.VMEM((whole, HD), f32),
            pltpu.VMEM((whole, HD), f32),
            pltpu.SemaphoreType.DMA((6,)),
            pltpu.SemaphoreType.DMA((n_span * n_g,)),
            pltpu.SemaphoreType.DMA,
            pltpu.SemaphoreType.DMA,
            pltpu.SemaphoreType.DMA,
            pltpu.SemaphoreType.DMA,
            pltpu.SemaphoreType.DMA,
            pltpu.SemaphoreType.DMA,
            pltpu.SemaphoreType.DMA,
            pltpu.SemaphoreType.DMA((n_g,)),
            pltpu.SemaphoreType.DMA,
            pltpu.SemaphoreType.DMA,
            pltpu.SemaphoreType.DMA,
        ],
        compiler_params=pltpu.CompilerParams(
            collective_id=0, has_side_effects=True, vmem_limit_bytes=VLIM * 2**20
        ),
        name="attention",
    )(queries, keys, values, timesteps.reshape(1, 1), history, gate_weight)


def solution(mesh):
    return jax.shard_map(
        body,
        mesh=mesh,
        in_specs=(
            P(("rep", "span"), "seq", None),
            P(("rep", "span"), "seq", None),
            P(("rep", "span"), "seq", None),
            P(("rep", "span")),
            P(("rep", "span"), None),
            P(None, "seq"),
        ),
        out_specs=P(("rep", "span"), "seq", None),
        check_vma=False,
    )
```

```python
import functools
import math

import jax
import jax.numpy as jnp
from jax import lax
from jax.experimental import pallas as pl
from jax.experimental.pallas import tpu as pltpu
from jax.sharding import PartitionSpec as P

HD = 128
FREQ = 256
RAISE = math.log2(math.e) / math.sqrt(HD)
HIDDEN = -1e30
VLIM = 60
WN = 2
GN = 4


def places(n_x, n_z, n_g):
    def far(p):
        return (min(p[1], n_z - p[1]), min(p[0], n_x - p[0]))

    def far_first(p):
        return (-far(p)[0], -far(p)[1], p)

    every = sorted(((a, b) for a in range(n_x) for b in range(n_z)), key=lambda p: (far(p), p))
    per = len(every) // n_g
    rest = sorted(every[per:], key=lambda p: (sum(far(p)), p))
    return every[:per] + sorted(rest[:per], key=far_first) + sorted(rest[per:], key=far_first)


def kernel(
    n_span, n_x, n_z, n_g, wrap, tok,
    q_hbm, k_hbm, v_hbm, steps_hbm, history_hbm, gatew_hbm,
    out_ref,
    q_in, k_in, v_in, steps, history, gatew, kv_stage, q_stage, kv, relay, qbuf, obuf, bias, gate_row, top, total, accum,
    in_sem, kv_recv, kv_send, direct_send, far_send, q_recv, q_send, down_send, side_send, wrap_send, relay_recv, relay_send, o_recv, o_send,
):
    n_seq = n_x * n_z
    n_direct = 1
    wrapped = range(n_direct, min(n_direct + WN, n_g)) if wrap else range(0)
    straight = range(n_direct + len(wrapped), n_g) if wrap else range(0)
    per = n_seq // n_g
    rows = per * tok
    n_chip = n_span // 2
    span, seq, video = lax.axis_index("span"), lax.axis_index("seq"), lax.axis_index("rep")
    chip, core = span // 2, lax.rem(span, 2)
    x, z = seq // n_z, lax.rem(seq, n_z)
    offsets = places(n_x, n_z, n_g)
    x_to = [lax.rem(x + d, n_x) * n_z for d in range(n_x)]
    z_to = [lax.rem(z + d, n_z) for d in range(n_z)]
    ahead = [x_to[a] + z_to[b] for a, b in offsets]
    behind = [x_to[(n_x - a) % n_x] + z_to[(n_z - b) % n_z] for a, b in offsets]
    slots = [(s, s // per, slice(s % per * tok, (s % per + 1) * tok)) for s in range(n_seq)]
    far_first = sorted(
        slots[1:],
        key=lambda s: tuple(-min(d, n - d) for d, n in zip(offsets[s[0]][::-1], (n_z, n_x))),
    )

    fetch = [
        pltpu.make_async_copy(src, dst, in_sem.at[i])
        for i, (src, dst) in enumerate((
            (k_hbm.at[0], k_in), (v_hbm.at[0], v_in), (q_hbm.at[0], q_in),
            (steps_hbm, steps), (history_hbm, history), (gatew_hbm, gatew),
        ))
    ]
    for copy in fetch:
        copy.start()
    barrier = pltpu.get_barrier_semaphore()
    sibling = span + 1 - 2 * core
    last = n_chip - 1
    hop1, hop2 = {"rep": 1 - video, "span": 2 + core}, {"rep": 1 - video, "span": 2 * last + core}

    def greet(to):
        pl.semaphore_signal(barrier, inc=1, device_id=to)

    for s, _, _ in far_first:
        greet({"seq": ahead[s]})
    greet({"span": sibling})
    pl.when(chip > 0)(lambda: greet({"span": span - 2}))
    pl.when(chip < last)(lambda: greet({"span": span + 2}))
    near = slots[:per]

    def greet_near(to):
        for s, _, _ in near[1:]:
            greet({**to, "seq": behind[s]})

    others = n_seq
    pl.when(chip > 0)(lambda: greet_near({"span": span - 2}))
    others += (per - 1) * (chip < last).astype(jnp.int32)
    others += (chip > 0).astype(jnp.int32) + (chip < last).astype(jnp.int32)
    if wrap:
        pl.when(chip == 0)(lambda: greet({"span": span + 2 * last}))
        pl.when(chip == last)(lambda: greet({"span": core}))
        pl.when(chip == last)(lambda: greet_near({"span": core}))
        others += (per - 1) * (chip == 0).astype(jnp.int32)
        pl.when(chip == 0)(lambda: greet(hop1))
        pl.when(chip == 1)(lambda: greet({"rep": 1 - video, "span": core}))
        pl.when(chip == 1)(lambda: greet(hop2))
        pl.when(chip == last)(lambda: greet(hop1))
        others += 2 * (1 - ((chip > 1) & (chip < last)).astype(jnp.int32))

    for copy, inputs, stage in zip(fetch, (k_in, v_in, q_in), (kv_stage.at[:, 0], kv_stage.at[:, 1], q_stage)):
        copy.wait()
        for t in range(n_seq):
            stage[t] = inputs[:, t * HD : (t + 1) * HD]
    kv[span * n_g, :, 0:tok, :] = kv_stage[seq]
    qbuf[0:tok, :] = q_stage[seq]
    pl.semaphore_wait(barrier, others)

    def send_near(to, sent):
        for s, g, at in near:
            pltpu.make_async_remote_copy(
                src_ref=kv_stage.at[ahead[s]],
                dst_ref=kv.at[span * n_g + g, :, at, :],
                send_sem=sent,
                recv_sem=kv_recv.at[span * n_g + g],
                device_id={"span": to, "seq": ahead[s]},
            ).start()

    pl.when(chip < last)(lambda: send_near(span + 2, direct_send))
    if wrap:
        pl.when(chip == 0)(lambda: send_near(span + 2 * last, far_send))
    for s, g, at in slots[1:]:
        pltpu.make_async_remote_copy(
            src_ref=kv_stage.at[ahead[s]],
            dst_ref=kv.at[span * n_g + g, :, at, :],
            send_sem=kv_send,
            recv_sem=kv_recv.at[span * n_g + g],
            device_id={"seq": ahead[s]},
        ).start()
    for s, _, _ in far_first:
        pltpu.make_async_remote_copy(
            src_ref=q_stage.at[ahead[s]],
            dst_ref=qbuf.at[s * tok : (s + 1) * tok, :],
            send_sem=q_send,
            recv_sem=q_recv,
            device_id={"seq": ahead[s]},
        ).start()

    for copy in fetch[3:]:
        copy.wait()
    n_freq = FREQ // 2
    k_index = lax.broadcasted_iota(jnp.int32, (8, n_freq), 1).astype(jnp.float32)
    freqs = jnp.exp(-math.log(10000.0) * k_index / n_freq)
    angle = steps[...].astype(jnp.float32) * freqs
    embedding = jnp.concatenate([jnp.cos(angle), jnp.sin(angle)], axis=-1).astype(jnp.bfloat16)
    gate_row[...] = jnp.dot(embedding, gatew[...], preferred_element_type=jnp.float32)

    n_block = n_span * n_seq
    spread = jnp.where(
        lax.broadcasted_iota(jnp.int32, (n_span, n_block), 1) // n_seq
        == lax.broadcasted_iota(jnp.int32, (n_span, n_block), 0),
        history[...],
        0,
    ).astype(jnp.float32).astype(jnp.bfloat16)
    key_slot = lax.broadcasted_iota(jnp.int32, (1, n_seq * tok), 1) // tok
    key_block = jnp.zeros(key_slot.shape, jnp.int32)
    for s in range(n_seq):
        key_block = jnp.where(key_slot == s, behind[s], key_block)
    place = lax.rem(lax.broadcasted_iota(jnp.int32, (n_block, n_seq * tok), 0), n_seq) == key_block
    shown = jnp.dot(
        spread, jnp.where(place, 1.0, 0.0).astype(jnp.bfloat16), preferred_element_type=jnp.float32
    )
    own = lax.broadcasted_iota(jnp.int32, shown.shape, 0) == span
    shade = jnp.where(own | (shown > 0.5), 0.0, HIDDEN)
    for part in range(2):
        bias[part] = shade[:, part * (n_g // 2 * rows) : (part + 1) * (n_g // 2 * rows)]
    top[...] = jnp.full(top.shape, HIDDEN, jnp.float32)
    total[...] = jnp.zeros(total.shape, jnp.float32)
    accum[...] = jnp.zeros(accum.shape, jnp.float32)

    def chunk_copy(j, g, sems, to):
        return pltpu.make_async_remote_copy(
            src_ref=kv.at[j * n_g + g],
            dst_ref=kv.at[j * n_g + g],
            send_sem=sems,
            recv_sem=kv_recv.at[j * n_g + g],
            device_id=to,
        )

    def wrap_copy(g):
        return pltpu.make_async_remote_copy(
            src_ref=kv.at[span * n_g + g],
            dst_ref=relay.at[g],
            send_sem=wrap_send,
            recv_sem=relay_recv.at[g],
            device_id=hop1,
        )

    def relay_copy(g):
        return pltpu.make_async_remote_copy(
            src_ref=relay.at[g],
            dst_ref=kv.at[core * n_g + g],
            send_sem=relay_send,
            recv_sem=kv_recv.at[core * n_g + g],
            device_id=hop2,
        )

    def goes_on(h):
        if wrap and h == last - 1:
            return chip < 0
        return chip < last

    def await_chunk(j, g, first=0):
        ref = kv.at[j * n_g + g, :, first:rows, :]
        pltpu.make_async_copy(ref, ref, kv_recv.at[j * n_g + g]).wait()

    half = n_g // 2

    def absorb(*pieces):
        wide = half * rows
        keys, values, shade = [], [], []
        for j, part in pieces:
            mine = pl.ds(j * n_g + part * half, half)
            keys.append(kv[mine, 0].reshape(wide, HD))
            values.append(kv[mine, 1].reshape(wide, HD))
            shade.append(bias[part, pl.ds(j, 1), :])
        scores = lax.dot_general(
            qbuf[...], jnp.concatenate(keys), (((1,), (1,)), ((), ())), preferred_element_type=jnp.float32
        )
        scores = scores + jnp.concatenate(shade, axis=1)
        largest = jnp.maximum(jnp.max(scores, axis=-1, keepdims=True), top[...])
        step = min(HD, 2 * wide)
        weights = [
            jnp.exp2((scores[:, a : a + step] - largest[:, :step]) * RAISE) for a in range(0, 2 * wide, step)
        ]
        added = functools.reduce(jnp.add, weights)
        weights = jnp.concatenate([w.astype(jnp.bfloat16) for w in weights], axis=1)
        summed = jnp.dot(weights, jnp.concatenate(values), preferred_element_type=jnp.float32)
        shrink = jnp.exp2((top[...] - largest) * RAISE)
        total[:, :step] = total[:, :step] * shrink[:, :step] + added
        accum[...] = accum[...] * shrink + summed
        top[...] = largest

    def take(h, g):
        j = span - 2 * h
        await_chunk(j, g)
        pl.when(goes_on(h))(chunk_copy(j, g, down_send, {"span": span + 2}).start)
        chunk_copy(j, g, side_send, {"span": sibling}).start()

    pl.when(chip > 0)(functools.partial(take, 1, 0))
    for g in range(n_g):
        if per > 1 or g > 0:
            await_chunk(span, g, tok if g == 0 else 0)
        if g >= n_direct:
            pl.when(goes_on(0))(chunk_copy(span, g, down_send, {"span": span + 2}).start)
        if g in wrapped:
            pl.when(chip == 0)(wrap_copy(g).start)
        pl.when(core == 0)(chunk_copy(span, g, side_send, {"span": sibling}).start)

    def halves(part):
        return range(part * half, (part + 1) * half)

    def do(op, *what):
        if op == "take":
            for g in halves(what[1]):
                if what[0] > 1 or g >= n_direct:
                    take(what[0], g)
        elif op == "side":
            for g in halves(what[1]):
                await_chunk(sibling - 2 * what[0], g)
        elif op == "relay":
            if what[0] in wrapped:
                here = relay.at[what[0]]
                pltpu.make_async_copy(here, here, relay_recv.at[what[0]]).wait()
                relay_copy(what[0]).start()
        elif op == "straight":
            for g in straight:
                chunk_copy(span, g, down_send, {"span": span + 2 * last}).start()
        elif op == "queries":
            rest = q_stage.at[1:n_seq]
            pltpu.make_async_copy(rest, rest, q_recv).wait()

    def plan(c, k):
        def take_both(h):
            return [("take", h, 0), ("take", h, 1)]

        def side_both(h):
            return [("side", h, 0), ("side", h, 1)]

        def whole(d):
            return [((d, 0), (d, 1))]

        def up(h):
            return whole(-2 * h)

        def side(h):
            return side_both(h) + whole(1 - 2 * k - 2 * h)

        def both_up(part):
            return [((-2 * (last - 1), part), (-2 * last, part))]

        def both_side(part):
            d = 1 - 2 * k
            return [("side", last - 1, part), ("side", last, part), ((d - 2 * (last - 1), part), (d - 2 * last, part))]

        start = [("queries",)] + whole(0)
        relays = [[("relay", g)] for g in wrapped] + [[]] * 4
        if c == 0:
            return start + (side(0) if k == 1 else []) + [("straight",)]
        if c == 1 and k == 0:
            return ([("take", 1, 0)] + start + relays[0] + [("take", 1, 1)] + relays[1] + side(1) + relays[2] + relays[3]
                    + up(1))
        if c == 1:
            return (take_both(1) + start + relays[0] + up(1) + relays[1] + side(0) + relays[2] + relays[3] + side(1))
        if c == 2 and k == 0:
            return ([("take", 1, 0)] + start + side(1) + [("take", 1, 1)] + up(1) + side(2) + take_both(2) + up(2))
        if c == 2:
            return take_both(1) + start + up(1) + side(0) + take_both(2) + up(2) + side(1) + side(2)
        if k == 0:
            return ([("take", 1, 0)] + start + side(1) + [("take", 1, 1)] + up(1)
                    + [("take", 2, 0)] + side(2) + [("take", 3, 0)] + both_up(0)
                    + [("take", 2, 1), ("take", 3, 1)] + side(3)
                    + both_up(1))
        return (take_both(1) + start + up(1) + side(0) + take_both(2) + up(2) + side(1) + take_both(3) + up(3)
                + both_side(0) + both_side(1))

    def run(c, k):
        steps, waits = [], []
        for one in plan(c, k):
            if isinstance(one[0], str):
                waits.append(one)
            else:
                steps.append((waits, one))
                waits = []

        @pl.loop(0, len(steps))
        def _(i):
            pieces = [[jnp.int32(0), jnp.int32(0)], [jnp.int32(0), jnp.int32(0)]]
            for n, (before, pair) in enumerate(steps):

                @pl.when(i == n)
                def _():
                    for one in before:
                        do(*one)

                for piece, (distance, part) in zip(pieces, pair):
                    piece[0] = jnp.where(i == n, distance, piece[0])
                    piece[1] = jnp.where(i == n, part, piece[1])
            absorb(*((span + distance, part) for distance, part in pieces))

        for one in waits:
            do(*one)

    for c in range(n_chip):
        for k in range(2):
            pl.when((chip == c) & (core == k))(functools.partial(run, c, k))

    for g in list(range(2, n_g)) + [1, 0]:
        at = slice(g * rows, (g + 1) * rows)
        whole = jnp.sum(total[at, : min(HD, n_g * rows)], axis=-1, keepdims=True)
        obuf[at, :] = (accum[at, :] * (1.0 / whole) * gate_row[0:1, :]).astype(jnp.bfloat16)
        for s, _, _ in far_first:
            if s // per == g:
                pltpu.make_async_remote_copy(
                    src_ref=obuf.at[s * tok : (s + 1) * tok, :],
                    dst_ref=out_ref.at[0, :, pl.ds(pl.multiple_of(seq * HD, HD), HD)],
                    send_sem=o_send,
                    recv_sem=o_recv,
                    device_id={"seq": behind[s]},
                ).start()
    mine = pltpu.make_async_copy(
        obuf.at[0:tok, :], out_ref.at[0, :, pl.ds(pl.multiple_of(seq * HD, HD), HD)], in_sem.at[0]
    )
    mine.start()
    mine.wait()

    def drain(ref, sem):
        pltpu.make_async_copy(ref, ref, sem).wait()

    drain(kv_stage.at[1:n_seq], kv_send)
    drain(q_stage.at[1:n_seq], q_send)
    pl.when(chip < last)(functools.partial(drain, kv_stage.at[0:per], direct_send))
    for c in range(n_chip):
        passed = [h for h in range(c + 1) if not (wrap and h == last - 1)] if c < last else []
        n_down = len(passed) * n_g - (n_direct if c < last else 0)
        n_down += len(straight) if c == 0 else 0
        if n_down:
            pl.when(chip == c)(functools.partial(drain, kv.at[0:n_down], down_send))
        pl.when((chip == c) & (core == 0))(functools.partial(drain, kv.at[0 : (c + 1) * n_g], side_send))
        if c > 0:
            pl.when((chip == c) & (core == 1))(functools.partial(drain, kv.at[0 : c * n_g], side_send))
    if wrap:
        if len(wrapped):
            pl.when(chip == 0)(functools.partial(drain, relay.at[0 : len(wrapped)], wrap_send))
            pl.when(chip == 1)(functools.partial(drain, relay.at[0 : len(wrapped)], relay_send))
        pl.when(chip == 0)(functools.partial(drain, kv_stage.at[0:per], far_send))
    drain(obuf.at[tok:, :], o_send)
    drain(out_ref.at[0, :, 0 : (n_seq - 1) * HD], o_recv)


def body(queries, keys, values, timesteps, history, gate_weight):
    n_span, n_seq = lax.axis_size("span"), lax.axis_size("seq")
    n_x = 4 if n_seq == 32 else 2
    n_z = n_seq // n_x
    n_g = GN if n_seq == 32 else 2
    wrap = n_span == 8 and lax.axis_size("rep") == 2
    tok, width = queries.shape[1], queries.shape[2]
    bf16, f32 = jnp.bfloat16, jnp.float32
    rows = n_seq // n_g * tok
    whole = n_seq * tok
    return pl.pallas_call(
        functools.partial(kernel, n_span, n_x, n_z, n_g, wrap, tok),
        out_shape=pltpu.VMEM(queries.shape, bf16),
        in_specs=[pl.BlockSpec(memory_space=pltpu.HBM)] * 6,
        out_specs=pl.BlockSpec(memory_space=pltpu.VMEM),
        scratch_shapes=[
            pltpu.VMEM((tok, width), bf16),
            pltpu.VMEM((tok, width), bf16),
            pltpu.VMEM((tok, width), bf16),
            pltpu.VMEM((1, 1), timesteps.dtype),
            pltpu.VMEM(history.shape, history.dtype),
            pltpu.VMEM(gate_weight.shape, bf16),
            pltpu.VMEM((n_seq, 2, tok, HD), bf16),
            pltpu.VMEM((n_seq, tok, HD), bf16),
            pltpu.VMEM((n_span * n_g, 2, rows, HD), bf16),
            pltpu.VMEM((n_g, 2, rows, HD), bf16),
            pltpu.VMEM((whole, HD), bf16),
            pltpu.VMEM((whole, HD), bf16),
            pltpu.VMEM((2, n_span, whole // 2), f32),
            pltpu.VMEM((8, HD), f32),
            pltpu.VMEM((whole, HD), f32),
            pltpu.VMEM((whole, HD), f32),
            pltpu.VMEM((whole, HD), f32),
            pltpu.SemaphoreType.DMA((6,)),
            pltpu.SemaphoreType.DMA((n_span * n_g,)),
            pltpu.SemaphoreType.DMA,
            pltpu.SemaphoreType.DMA,
            pltpu.SemaphoreType.DMA,
            pltpu.SemaphoreType.DMA,
            pltpu.SemaphoreType.DMA,
            pltpu.SemaphoreType.DMA,
            pltpu.SemaphoreType.DMA,
            pltpu.SemaphoreType.DMA,
            pltpu.SemaphoreType.DMA((n_g,)),
            pltpu.SemaphoreType.DMA,
            pltpu.SemaphoreType.DMA,
            pltpu.SemaphoreType.DMA,
        ],
        compiler_params=pltpu.CompilerParams(
            collective_id=0, has_side_effects=True, vmem_limit_bytes=VLIM * 2**20
        ),
        name="attention",
    )(queries, keys, values, timesteps.reshape(1, 1), history, gate_weight)


def solution(mesh):
    return jax.shard_map(
        body,
        mesh=mesh,
        in_specs=(
            P(("rep", "span"), "seq", None),
            P(("rep", "span"), "seq", None),
            P(("rep", "span"), "seq", None),
            P(("rep", "span")),
            P(("rep", "span"), None),
            P(None, "seq"),
        ),
        out_specs=P(("rep", "span"), "seq", None),
        check_vma=False,
    )
```

```python
import functools
import math

import jax
import jax.numpy as jnp
from jax import lax
from jax.experimental import pallas as pl
from jax.experimental.pallas import tpu as pltpu
from jax.sharding import PartitionSpec as P

HD = 128
FREQ = 256
RAISE = math.log2(math.e) / math.sqrt(HD)
HIDDEN = -1e30
VLIM = 60
WN = 2
GN = 4


def places(n_x, n_z, n_g):
    def far(p):
        return (min(p[1], n_z - p[1]), min(p[0], n_x - p[0]))

    def far_first(p):
        return (-far(p)[0], -far(p)[1], p)

    every = sorted(((a, b) for a in range(n_x) for b in range(n_z)), key=lambda p: (far(p), p))
    per = len(every) // n_g
    rest = sorted(every[per:], key=lambda p: (sum(far(p)), p))
    return every[:per] + sorted(rest[:per], key=far_first) + sorted(rest[per:], key=far_first)


def kernel(
    n_span, n_x, n_z, n_g, wrap, tok,
    q_hbm, k_hbm, v_hbm, steps_hbm, history_hbm, gatew_hbm,
    out_ref,
    q_in, k_in, v_in, steps, history, gatew, kv_stage, q_stage, kv, relay, qbuf, obuf, bias, gate_row, top, total, accum,
    in_sem, kv_recv, kv_send, direct_send, far_send, q_recv, q_send, down_send, side_send, wrap_send, relay_recv, relay_send, o_recv, o_send,
):
    n_seq = n_x * n_z
    n_direct = 1
    wrapped = range(n_direct, min(n_direct + WN, n_g)) if wrap else range(0)
    straight = range(n_direct + len(wrapped), n_g) if wrap else range(0)
    per = n_seq // n_g
    rows = per * tok
    n_chip = n_span // 2
    span, seq, video = lax.axis_index("span"), lax.axis_index("seq"), lax.axis_index("rep")
    chip, core = span // 2, lax.rem(span, 2)
    x, z = seq // n_z, lax.rem(seq, n_z)
    offsets = places(n_x, n_z, n_g)
    x_to = [lax.rem(x + d, n_x) * n_z for d in range(n_x)]
    z_to = [lax.rem(z + d, n_z) for d in range(n_z)]
    ahead = [x_to[a] + z_to[b] for a, b in offsets]
    behind = [x_to[(n_x - a) % n_x] + z_to[(n_z - b) % n_z] for a, b in offsets]
    slots = [(s, s // per, slice(s % per * tok, (s % per + 1) * tok)) for s in range(n_seq)]
    far_first = sorted(
        slots[1:],
        key=lambda s: tuple(-min(d, n - d) for d, n in zip(offsets[s[0]][::-1], (n_z, n_x))),
    )

    fetch = [
        pltpu.make_async_copy(src, dst, in_sem.at[i])
        for i, (src, dst) in enumerate((
            (k_hbm.at[0], k_in), (v_hbm.at[0], v_in), (q_hbm.at[0], q_in),
            (steps_hbm, steps), (history_hbm, history), (gatew_hbm, gatew),
        ))
    ]
    for copy in fetch:
        copy.start()
    barrier = pltpu.get_barrier_semaphore()
    sibling = span + 1 - 2 * core
    last = n_chip - 1
    hop1, hop2 = {"rep": 1 - video, "span": 2 + core}, {"rep": 1 - video, "span": 2 * last + core}

    def greet(to):
        pl.semaphore_signal(barrier, inc=1, device_id=to)

    for s, _, _ in far_first:
        greet({"seq": ahead[s]})
    greet({"span": sibling})
    pl.when(chip > 0)(lambda: greet({"span": span - 2}))
    pl.when(chip < last)(lambda: greet({"span": span + 2}))
    near = slots[:per]

    def greet_near(to):
        for s, _, _ in near[1:]:
            greet({**to, "seq": behind[s]})

    others = n_seq
    pl.when(chip > 0)(lambda: greet_near({"span": span - 2}))
    others += (per - 1) * (chip < last).astype(jnp.int32)
    others += (chip > 0).astype(jnp.int32) + (chip < last).astype(jnp.int32)
    if wrap:
        pl.when(chip == 0)(lambda: greet({"span": span + 2 * last}))
        pl.when(chip == last)(lambda: greet({"span": core}))
        pl.when(chip == last)(lambda: greet_near({"span": core}))
        others += (per - 1) * (chip == 0).astype(jnp.int32)
        pl.when(chip == 0)(lambda: greet(hop1))
        pl.when(chip == 1)(lambda: greet({"rep": 1 - video, "span": core}))
        pl.when(chip == 1)(lambda: greet(hop2))
        pl.when(chip == last)(lambda: greet(hop1))
        others += 2 * (1 - ((chip > 1) & (chip < last)).astype(jnp.int32))

    for copy, inputs, stage in zip(fetch, (k_in, v_in, q_in), (kv_stage.at[:, 0], kv_stage.at[:, 1], q_stage)):
        copy.wait()
        for t in range(n_seq):
            stage[t] = inputs[:, t * HD : (t + 1) * HD]
    kv[span * n_g, :, 0:tok, :] = kv_stage[seq]
    qbuf[0:tok, :] = q_stage[seq]
    pl.semaphore_wait(barrier, others)

    def send_near(to, sent):
        for s, g, at in near:
            pltpu.make_async_remote_copy(
                src_ref=kv_stage.at[ahead[s]],
                dst_ref=kv.at[span * n_g + g, :, at, :],
                send_sem=sent,
                recv_sem=kv_recv.at[span * n_g + g],
                device_id={"span": to, "seq": ahead[s]},
            ).start()

    pl.when(chip < last)(lambda: send_near(span + 2, direct_send))
    if wrap:
        pl.when(chip == 0)(lambda: send_near(span + 2 * last, far_send))
    for s, g, at in slots[1:]:
        pltpu.make_async_remote_copy(
            src_ref=kv_stage.at[ahead[s]],
            dst_ref=kv.at[span * n_g + g, :, at, :],
            send_sem=kv_send,
            recv_sem=kv_recv.at[span * n_g + g],
            device_id={"seq": ahead[s]},
        ).start()
    for s, _, _ in far_first:
        pltpu.make_async_remote_copy(
            src_ref=q_stage.at[ahead[s]],
            dst_ref=qbuf.at[s * tok : (s + 1) * tok, :],
            send_sem=q_send,
            recv_sem=q_recv,
            device_id={"seq": ahead[s]},
        ).start()

    for copy in fetch[3:]:
        copy.wait()
    n_freq = FREQ // 2
    k_index = lax.broadcasted_iota(jnp.int32, (8, n_freq), 1).astype(jnp.float32)
    freqs = jnp.exp(-math.log(10000.0) * k_index / n_freq)
    angle = steps[0].astype(jnp.float32) * freqs
    embedding = jnp.concatenate([jnp.cos(angle), jnp.sin(angle)], axis=-1).astype(jnp.bfloat16)
    gate_row[...] = jnp.dot(embedding, gatew[...], preferred_element_type=jnp.float32)

    n_block = n_span * n_seq
    spread = jnp.where(
        lax.broadcasted_iota(jnp.int32, (n_span, n_block), 1) // n_seq
        == lax.broadcasted_iota(jnp.int32, (n_span, n_block), 0),
        history[...],
        0,
    ).astype(jnp.float32).astype(jnp.bfloat16)
    key_slot = lax.broadcasted_iota(jnp.int32, (1, n_seq * tok), 1) // tok
    key_block = jnp.zeros(key_slot.shape, jnp.int32)
    for s in range(n_seq):
        key_block = jnp.where(key_slot == s, behind[s], key_block)
    place = lax.rem(lax.broadcasted_iota(jnp.int32, (n_block, n_seq * tok), 0), n_seq) == key_block
    shown = jnp.dot(
        spread, jnp.where(place, 1.0, 0.0).astype(jnp.bfloat16), preferred_element_type=jnp.float32
    )
    own = lax.broadcasted_iota(jnp.int32, shown.shape, 0) == span
    shade = jnp.where(own | (shown > 0.5), 0.0, HIDDEN)
    for part in range(2):
        bias[part] = shade[:, part * (n_g // 2 * rows) : (part + 1) * (n_g // 2 * rows)]
    top[...] = jnp.full(top.shape, HIDDEN, jnp.float32)
    total[...] = jnp.zeros(total.shape, jnp.float32)
    accum[...] = jnp.zeros(accum.shape, jnp.float32)

    def chunk_copy(j, g, sems, to):
        return pltpu.make_async_remote_copy(
            src_ref=kv.at[j * n_g + g],
            dst_ref=kv.at[j * n_g + g],
            send_sem=sems,
            recv_sem=kv_recv.at[j * n_g + g],
            device_id=to,
        )

    def wrap_copy(g):
        return pltpu.make_async_remote_copy(
            src_ref=kv.at[span * n_g + g],
            dst_ref=relay.at[g],
            send_sem=wrap_send,
            recv_sem=relay_recv.at[g],
            device_id=hop1,
        )

    def relay_copy(g):
        return pltpu.make_async_remote_copy(
            src_ref=relay.at[g],
            dst_ref=kv.at[core * n_g + g],
            send_sem=relay_send,
            recv_sem=kv_recv.at[core * n_g + g],
            device_id=hop2,
        )

    def goes_on(h):
        if wrap and h == last - 1:
            return chip < 0
        return chip < last

    def await_chunk(j, g, first=0):
        ref = kv.at[j * n_g + g, :, first:rows, :]
        pltpu.make_async_copy(ref, ref, kv_recv.at[j * n_g + g]).wait()

    half = n_g // 2

    def absorb(*pieces):
        wide = half * rows
        keys, values, shade = [], [], []
        for j, part in pieces:
            mine = pl.ds(j * n_g + part * half, half)
            keys.append(kv[mine, 0].reshape(wide, HD))
            values.append(kv[mine, 1].reshape(wide, HD))
            shade.append(bias[part, pl.ds(j, 1), :])
        scores = lax.dot_general(
            qbuf[...], jnp.concatenate(keys), (((1,), (1,)), ((), ())), preferred_element_type=jnp.float32
        )
        scores = scores + jnp.concatenate(shade, axis=1)
        largest = jnp.maximum(jnp.max(scores, axis=-1, keepdims=True), top[...])
        step = min(HD, 2 * wide)
        weights = [
            jnp.exp2((scores[:, a : a + step] - largest[:, :step]) * RAISE) for a in range(0, 2 * wide, step)
        ]
        added = functools.reduce(jnp.add, weights)
        weights = jnp.concatenate([w.astype(jnp.bfloat16) for w in weights], axis=1)
        summed = jnp.dot(weights, jnp.concatenate(values), preferred_element_type=jnp.float32)
        shrink = jnp.exp2((top[...] - largest) * RAISE)
        total[:, :step] = total[:, :step] * shrink[:, :step] + added
        accum[...] = accum[...] * shrink + summed
        top[...] = largest

    def take(h, g):
        j = span - 2 * h
        await_chunk(j, g)
        pl.when(goes_on(h))(chunk_copy(j, g, down_send, {"span": span + 2}).start)
        chunk_copy(j, g, side_send, {"span": sibling}).start()

    pl.when(chip > 0)(functools.partial(take, 1, 0))
    for g in range(n_g):
        if per > 1 or g > 0:
            await_chunk(span, g, tok if g == 0 else 0)
        if g >= n_direct:
            pl.when(goes_on(0))(chunk_copy(span, g, down_send, {"span": span + 2}).start)
        if g in wrapped:
            pl.when(chip == 0)(wrap_copy(g).start)
        pl.when(core == 0)(chunk_copy(span, g, side_send, {"span": sibling}).start)

    def halves(part):
        return range(part * half, (part + 1) * half)

    def do(op, *what):
        if op == "take":
            for g in halves(what[1]):
                if what[0] > 1 or g >= n_direct:
                    take(what[0], g)
        elif op == "side":
            for g in halves(what[1]):
                await_chunk(sibling - 2 * what[0], g)
        elif op == "relay":
            if what[0] in wrapped:
                here = relay.at[what[0]]
                pltpu.make_async_copy(here, here, relay_recv.at[what[0]]).wait()
                relay_copy(what[0]).start()
        elif op == "straight":
            for g in straight:
                chunk_copy(span, g, down_send, {"span": span + 2 * last}).start()
        elif op == "queries":
            rest = q_stage.at[1:n_seq]
            pltpu.make_async_copy(rest, rest, q_recv).wait()

    def plan(c, k):
        def take_both(h):
            return [("take", h, 0), ("take", h, 1)]

        def side_both(h):
            return [("side", h, 0), ("side", h, 1)]

        def whole(d):
            return [((d, 0), (d, 1))]

        def up(h):
            return whole(-2 * h)

        def side(h):
            return side_both(h) + whole(1 - 2 * k - 2 * h)

        def both_up(part):
            return [((-2 * (last - 1), part), (-2 * last, part))]

        def both_side(part):
            d = 1 - 2 * k
            return [("side", last - 1, part), ("side", last, part), ((d - 2 * (last - 1), part), (d - 2 * last, part))]

        start = [("queries",)] + whole(0)
        relays = [[("relay", g)] for g in wrapped] + [[]] * 4
        if c == 0:
            return start + (side(0) if k == 1 else []) + [("straight",)]
        if c == 1 and k == 0:
            return ([("take", 1, 0)] + start + relays[0] + [("take", 1, 1)] + relays[1] + side(1) + relays[2] + relays[3]
                    + up(1))
        if c == 1:
            return (take_both(1) + start + relays[0] + up(1) + relays[1] + side(0) + relays[2] + relays[3] + side(1))
        if c == 2 and k == 0:
            return ([("take", 1, 0)] + start + side(1) + [("take", 1, 1)] + up(1) + side(2) + take_both(2) + up(2))
        if c == 2:
            return take_both(1) + start + up(1) + side(0) + take_both(2) + up(2) + side(1) + side(2)
        if k == 0:
            return ([("take", 1, 0)] + start + side(1) + [("take", 1, 1)] + up(1)
                    + [("take", 2, 0)] + side(2) + [("take", 3, 0)] + both_up(0)
                    + [("take", 2, 1), ("take", 3, 1)] + side(3)
                    + both_up(1))
        return (take_both(1) + start + up(1) + side(0) + take_both(2) + up(2) + side(1) + take_both(3) + up(3)
                + both_side(0) + both_side(1))

    def run(c, k):
        steps, waits = [], []
        for one in plan(c, k):
            if isinstance(one[0], str):
                waits.append(one)
            else:
                steps.append((waits, one))
                waits = []

        @pl.loop(0, len(steps))
        def _(i):
            pieces = [[jnp.int32(0), jnp.int32(0)], [jnp.int32(0), jnp.int32(0)]]
            for n, (before, pair) in enumerate(steps):

                @pl.when(i == n)
                def _():
                    for one in before:
                        do(*one)

                for piece, (distance, part) in zip(pieces, pair):
                    piece[0] = jnp.where(i == n, distance, piece[0])
                    piece[1] = jnp.where(i == n, part, piece[1])
            absorb(*((span + distance, part) for distance, part in pieces))

        for one in waits:
            do(*one)

    for c in range(n_chip):
        for k in range(2):
            pl.when((chip == c) & (core == k))(functools.partial(run, c, k))

    for g in list(range(2, n_g)) + [1, 0]:
        at = slice(g * rows, (g + 1) * rows)
        whole = jnp.sum(total[at, : min(HD, n_g * rows)], axis=-1, keepdims=True)
        obuf[at, :] = (accum[at, :] * (1.0 / whole) * gate_row[0:1, :]).astype(jnp.bfloat16)
        for s, _, _ in far_first:
            if s // per == g:
                pltpu.make_async_remote_copy(
                    src_ref=obuf.at[s * tok : (s + 1) * tok, :],
                    dst_ref=out_ref.at[0, :, pl.ds(pl.multiple_of(seq * HD, HD), HD)],
                    send_sem=o_send,
                    recv_sem=o_recv,
                    device_id={"seq": behind[s]},
                ).start()
    mine = pltpu.make_async_copy(
        obuf.at[0:tok, :], out_ref.at[0, :, pl.ds(pl.multiple_of(seq * HD, HD), HD)], in_sem.at[0]
    )
    mine.start()
    mine.wait()

    def drain(ref, sem):
        pltpu.make_async_copy(ref, ref, sem).wait()

    drain(kv_stage.at[1:n_seq], kv_send)
    drain(q_stage.at[1:n_seq], q_send)
    pl.when(chip < last)(functools.partial(drain, kv_stage.at[0:per], direct_send))
    for c in range(n_chip):
        passed = [h for h in range(c + 1) if not (wrap and h == last - 1)] if c < last else []
        n_down = len(passed) * n_g - (n_direct if c < last else 0)
        n_down += len(straight) if c == 0 else 0
        if n_down:
            pl.when(chip == c)(functools.partial(drain, kv.at[0:n_down], down_send))
        pl.when((chip == c) & (core == 0))(functools.partial(drain, kv.at[0 : (c + 1) * n_g], side_send))
        if c > 0:
            pl.when((chip == c) & (core == 1))(functools.partial(drain, kv.at[0 : c * n_g], side_send))
    if wrap:
        if len(wrapped):
            pl.when(chip == 0)(functools.partial(drain, relay.at[0 : len(wrapped)], wrap_send))
            pl.when(chip == 1)(functools.partial(drain, relay.at[0 : len(wrapped)], relay_send))
        pl.when(chip == 0)(functools.partial(drain, kv_stage.at[0:per], far_send))
    drain(obuf.at[tok:, :], o_send)
    drain(out_ref.at[0, :, 0 : (n_seq - 1) * HD], o_recv)


def body(queries, keys, values, timesteps, history, gate_weight):
    n_span, n_seq = lax.axis_size("span"), lax.axis_size("seq")
    n_x = 4 if n_seq == 32 else 2
    n_z = n_seq // n_x
    n_g = GN if n_seq == 32 else 2
    wrap = n_span == 8 and lax.axis_size("rep") == 2
    tok, width = queries.shape[1], queries.shape[2]
    bf16, f32 = jnp.bfloat16, jnp.float32
    rows = n_seq // n_g * tok
    whole = n_seq * tok
    return pl.pallas_call(
        functools.partial(kernel, n_span, n_x, n_z, n_g, wrap, tok),
        out_shape=pltpu.VMEM(queries.shape, bf16),
        in_specs=[pl.BlockSpec(memory_space=pl.ANY)] * 6,
        out_specs=pl.BlockSpec(memory_space=pltpu.VMEM),
        scratch_shapes=[
            pltpu.VMEM((tok, width), bf16),
            pltpu.VMEM((tok, width), bf16),
            pltpu.VMEM((tok, width), bf16),
            pltpu.SMEM(timesteps.shape, timesteps.dtype),
            pltpu.VMEM(history.shape, history.dtype),
            pltpu.VMEM(gate_weight.shape, bf16),
            pltpu.VMEM((n_seq, 2, tok, HD), bf16),
            pltpu.VMEM((n_seq, tok, HD), bf16),
            pltpu.VMEM((n_span * n_g, 2, rows, HD), bf16),
            pltpu.VMEM((n_g, 2, rows, HD), bf16),
            pltpu.VMEM((whole, HD), bf16),
            pltpu.VMEM((whole, HD), bf16),
            pltpu.VMEM((2, n_span, whole // 2), f32),
            pltpu.VMEM((8, HD), f32),
            pltpu.VMEM((whole, HD), f32),
            pltpu.VMEM((whole, HD), f32),
            pltpu.VMEM((whole, HD), f32),
            pltpu.SemaphoreType.DMA((6,)),
            pltpu.SemaphoreType.DMA((n_span * n_g,)),
            pltpu.SemaphoreType.DMA,
            pltpu.SemaphoreType.DMA,
            pltpu.SemaphoreType.DMA,
            pltpu.SemaphoreType.DMA,
            pltpu.SemaphoreType.DMA,
            pltpu.SemaphoreType.DMA,
            pltpu.SemaphoreType.DMA,
            pltpu.SemaphoreType.DMA,
            pltpu.SemaphoreType.DMA((n_g,)),
            pltpu.SemaphoreType.DMA,
            pltpu.SemaphoreType.DMA,
            pltpu.SemaphoreType.DMA,
        ],
        compiler_params=pltpu.CompilerParams(
            collective_id=0, has_side_effects=True, vmem_limit_bytes=VLIM * 2**20
        ),
        name="attention",
    )(queries, keys, values, timesteps, history, gate_weight)


def solution(mesh):
    return jax.shard_map(
        body,
        mesh=mesh,
        in_specs=(
            P(("rep", "span"), "seq", None),
            P(("rep", "span"), "seq", None),
            P(("rep", "span"), "seq", None),
            P(("rep", "span")),
            P(("rep", "span"), None),
            P(None, "seq"),
        ),
        out_specs=P(("rep", "span"), "seq", None),
        check_vma=False,
    )
```

```python
import functools
import math

import jax
import jax.numpy as jnp
from jax import lax
from jax.experimental import pallas as pl
from jax.experimental.pallas import tpu as pltpu
from jax.sharding import PartitionSpec as P

HD = 128
FREQ = 256
RAISE = math.log2(math.e) / math.sqrt(HD)
HIDDEN = -1e30
VLIM = 60
WN = 2
GN = 4


def places(n_x, n_z, n_g):
    def far(p):
        return (min(p[1], n_z - p[1]), min(p[0], n_x - p[0]))

    def far_first(p):
        return (-far(p)[0], -far(p)[1], p)

    every = sorted(((a, b) for a in range(n_x) for b in range(n_z)), key=lambda p: (far(p), p))
    per = len(every) // n_g
    rest = sorted(every[per:], key=lambda p: (sum(far(p)), p))
    return every[:per] + sorted(rest[:per], key=far_first) + sorted(rest[per:], key=far_first)


def kernel(
    n_span, n_x, n_z, n_g, wrap, tok,
    q_hbm, k_hbm, v_hbm, steps_hbm, history_hbm, gatew_hbm,
    out_ref,
    q_in, k_in, v_in, steps, history, gatew, kv_stage, q_stage, kv, relay, qbuf, obuf, bias, gate_row, top, total, accum,
    in_sem, kv_recv, kv_send, direct_send, far_send, q_recv, q_send, down_send, side_send, wrap_send, relay_recv, relay_send, o_recv, o_send,
):
    n_seq = n_x * n_z
    n_direct = 1
    wrapped = range(n_direct, min(n_direct + WN, n_g)) if wrap else range(0)
    straight = range(n_direct + len(wrapped), n_g) if wrap else range(0)
    per = n_seq // n_g
    rows = per * tok
    n_chip = n_span // 2
    span, seq, video = lax.axis_index("span"), lax.axis_index("seq"), lax.axis_index("rep")
    chip, core = span // 2, lax.rem(span, 2)
    x, z = seq // n_z, lax.rem(seq, n_z)
    offsets = places(n_x, n_z, n_g)
    x_to = [lax.rem(x + d, n_x) * n_z for d in range(n_x)]
    z_to = [lax.rem(z + d, n_z) for d in range(n_z)]
    ahead = [x_to[a] + z_to[b] for a, b in offsets]
    behind = [x_to[(n_x - a) % n_x] + z_to[(n_z - b) % n_z] for a, b in offsets]
    slots = [(s, s // per, slice(s % per * tok, (s % per + 1) * tok)) for s in range(n_seq)]
    far_first = sorted(
        slots[1:],
        key=lambda s: tuple(-min(d, n - d) for d, n in zip(offsets[s[0]][::-1], (n_z, n_x))),
    )

    fetch = [
        pltpu.make_async_copy(src, dst, in_sem.at[i])
        for i, (src, dst) in enumerate((
            (k_hbm.at[0], k_in), (v_hbm.at[0], v_in), (q_hbm.at[0], q_in),
            (steps_hbm, steps), (history_hbm, history), (gatew_hbm, gatew),
        ))
    ]
    for copy in fetch:
        copy.start()
    barrier = pltpu.get_barrier_semaphore()
    sibling = span + 1 - 2 * core
    last = n_chip - 1
    hop1, hop2 = {"rep": 1 - video, "span": 2 + core}, {"rep": 1 - video, "span": 2 * last + core}

    def greet(to):
        pl.semaphore_signal(barrier, inc=1, device_id=to)

    for s, _, _ in far_first:
        greet({"seq": ahead[s]})
    greet({"span": sibling})
    pl.when(chip > 0)(lambda: greet({"span": span - 2}))
    pl.when(chip < last)(lambda: greet({"span": span + 2}))
    near = slots[:per]

    def greet_near(to):
        for s, _, _ in near[1:]:
            greet({**to, "seq": behind[s]})

    others = n_seq
    pl.when(chip > 0)(lambda: greet_near({"span": span - 2}))
    others += (per - 1) * (chip < last).astype(jnp.int32)
    others += (chip > 0).astype(jnp.int32) + (chip < last).astype(jnp.int32)
    if wrap:
        pl.when(chip == 0)(lambda: greet({"span": span + 2 * last}))
        pl.when(chip == last)(lambda: greet({"span": core}))
        pl.when(chip == last)(lambda: greet_near({"span": core}))
        others += (per - 1) * (chip == 0).astype(jnp.int32)
        pl.when(chip == 0)(lambda: greet(hop1))
        pl.when(chip == 1)(lambda: greet({"rep": 1 - video, "span": core}))
        pl.when(chip == 1)(lambda: greet(hop2))
        pl.when(chip == last)(lambda: greet(hop1))
        others += 2 * (1 - ((chip > 1) & (chip < last)).astype(jnp.int32))

    for copy, inputs, stage in zip(fetch, (k_in, v_in, q_in), (kv_stage.at[:, 0], kv_stage.at[:, 1], q_stage)):
        copy.wait()
        for t in range(n_seq):
            stage[t] = inputs[:, t * HD : (t + 1) * HD]
    kv[span * n_g, :, 0:tok, :] = kv_stage[seq]
    qbuf[0:tok, :] = q_stage[seq]
    pl.semaphore_wait(barrier, others)

    def send_near(to, sent):
        for s, g, at in near:
            pltpu.make_async_remote_copy(
                src_ref=kv_stage.at[ahead[s]],
                dst_ref=kv.at[span * n_g + g, :, at, :],
                send_sem=sent,
                recv_sem=kv_recv.at[span * n_g + g],
                device_id={"span": to, "seq": ahead[s]},
            ).start()

    pl.when(chip < last)(lambda: send_near(span + 2, direct_send))
    if wrap:
        pl.when(chip == 0)(lambda: send_near(span + 2 * last, far_send))
    for s, g, at in slots[1:]:
        pltpu.make_async_remote_copy(
            src_ref=kv_stage.at[ahead[s]],
            dst_ref=kv.at[span * n_g + g, :, at, :],
            send_sem=kv_send,
            recv_sem=kv_recv.at[span * n_g + g],
            device_id={"seq": ahead[s]},
        ).start()
    for s, _, _ in far_first:
        pltpu.make_async_remote_copy(
            src_ref=q_stage.at[ahead[s]],
            dst_ref=qbuf.at[s * tok : (s + 1) * tok, :],
            send_sem=q_send,
            recv_sem=q_recv,
            device_id={"seq": ahead[s]},
        ).start()

    for copy in fetch[3:]:
        copy.wait()
    n_freq = FREQ // 2
    k_index = lax.broadcasted_iota(jnp.int32, (8, n_freq), 1).astype(jnp.float32)
    freqs = jnp.exp(-math.log(10000.0) * k_index / n_freq)
    angle = steps[0].astype(jnp.float32) * freqs
    embedding = jnp.concatenate([jnp.cos(angle), jnp.sin(angle)], axis=-1).astype(jnp.bfloat16)
    gate_row[...] = jnp.dot(embedding, gatew[...], preferred_element_type=jnp.float32)

    n_block = n_span * n_seq
    spread = jnp.where(
        lax.broadcasted_iota(jnp.int32, (n_span, n_block), 1) // n_seq
        == lax.broadcasted_iota(jnp.int32, (n_span, n_block), 0),
        history[...],
        0,
    ).astype(jnp.float32).astype(jnp.bfloat16)
    key_slot = lax.broadcasted_iota(jnp.int32, (1, n_seq * tok), 1) // tok
    key_block = jnp.zeros(key_slot.shape, jnp.int32)
    for s in range(n_seq):
        key_block = jnp.where(key_slot == s, behind[s], key_block)
    place = lax.rem(lax.broadcasted_iota(jnp.int32, (n_block, n_seq * tok), 0), n_seq) == key_block
    shown = jnp.dot(
        spread, jnp.where(place, 1.0, 0.0).astype(jnp.bfloat16), preferred_element_type=jnp.float32
    )
    own = lax.broadcasted_iota(jnp.int32, shown.shape, 0) == span
    shade = jnp.where(own | (shown > 0.5), 0.0, HIDDEN)
    for part in range(2):
        bias[part] = shade[:, part * (n_g // 2 * rows) : (part + 1) * (n_g // 2 * rows)]
    top[...] = jnp.full(top.shape, HIDDEN, jnp.float32)
    total[...] = jnp.zeros(total.shape, jnp.float32)
    accum[...] = jnp.zeros(accum.shape, jnp.float32)

    def chunk_copy(j, g, sems, to):
        return pltpu.make_async_remote_copy(
            src_ref=kv.at[j * n_g + g],
            dst_ref=kv.at[j * n_g + g],
            send_sem=sems,
            recv_sem=kv_recv.at[j * n_g + g],
            device_id=to,
        )

    def wrap_copy(g):
        return pltpu.make_async_remote_copy(
            src_ref=kv.at[span * n_g + g],
            dst_ref=relay.at[g],
            send_sem=wrap_send,
            recv_sem=relay_recv.at[g],
            device_id=hop1,
        )

    def relay_copy(g):
        return pltpu.make_async_remote_copy(
            src_ref=relay.at[g],
            dst_ref=kv.at[core * n_g + g],
            send_sem=relay_send,
            recv_sem=kv_recv.at[core * n_g + g],
            device_id=hop2,
        )

    def goes_on(h):
        if wrap and h == last - 1:
            return chip < 0
        return chip < last

    def await_chunk(j, g, first=0):
        ref = kv.at[j * n_g + g, :, first:rows, :]
        pltpu.make_async_copy(ref, ref, kv_recv.at[j * n_g + g]).wait()

    half = n_g // 2

    def absorb(*pieces):
        wide = half * rows
        keys, values, shade = [], [], []
        for j, part in pieces:
            mine = pl.ds(j * n_g + part * half, half)
            keys.append(kv[mine, 0].reshape(wide, HD))
            values.append(kv[mine, 1].reshape(wide, HD))
            shade.append(bias[part, pl.ds(j, 1), :])
        scores = lax.dot_general(
            qbuf[...], jnp.concatenate(keys), (((1,), (1,)), ((), ())), preferred_element_type=jnp.float32
        )
        scores = scores + jnp.concatenate(shade, axis=1)
        largest = jnp.maximum(jnp.max(scores, axis=-1, keepdims=True), top[...])
        step = min(HD, 2 * wide)
        weights = [
            jnp.exp2((scores[:, a : a + step] - largest[:, :step]) * RAISE) for a in range(0, 2 * wide, step)
        ]
        added = functools.reduce(jnp.add, weights)
        weights = jnp.concatenate([w.astype(jnp.bfloat16) for w in weights], axis=1)
        summed = jnp.dot(weights, jnp.concatenate(values), preferred_element_type=jnp.float32)
        shrink = jnp.exp2((top[...] - largest) * RAISE)
        total[:, :step] = total[:, :step] * shrink[:, :step] + added
        accum[...] = accum[...] * shrink + summed
        top[...] = largest

    def take(h, g):
        j = span - 2 * h
        await_chunk(j, g)
        pl.when(goes_on(h))(chunk_copy(j, g, down_send, {"span": span + 2}).start)
        chunk_copy(j, g, side_send, {"span": sibling}).start()

    pl.when(chip > 0)(functools.partial(take, 1, 0))
    for g in range(n_g):
        if per > 1 or g > 0:
            await_chunk(span, g, tok if g == 0 else 0)
        if g >= n_direct:
            pl.when(goes_on(0))(chunk_copy(span, g, down_send, {"span": span + 2}).start)
        if g in wrapped:
            pl.when(chip == 0)(wrap_copy(g).start)
        pl.when(core == 0)(chunk_copy(span, g, side_send, {"span": sibling}).start)

    def halves(part):
        return range(part * half, (part + 1) * half)

    def do(op, *what):
        if op == "take":
            for g in halves(what[1]):
                if what[0] > 1 or g >= n_direct:
                    take(what[0], g)
        elif op == "side":
            for g in halves(what[1]):
                await_chunk(sibling - 2 * what[0], g)
        elif op == "relay":
            if what[0] in wrapped:
                here = relay.at[what[0]]
                pltpu.make_async_copy(here, here, relay_recv.at[what[0]]).wait()
                relay_copy(what[0]).start()
        elif op == "straight":
            for g in straight:
                chunk_copy(span, g, down_send, {"span": span + 2 * last}).start()
        elif op == "queries":
            rest = q_stage.at[1:n_seq]
            pltpu.make_async_copy(rest, rest, q_recv).wait()

    def plan(c, k):
        def take_both(h):
            return [("take", h, 0), ("take", h, 1)]

        def side_both(h):
            return [("side", h, 0), ("side", h, 1)]

        def whole(d):
            return [((d, 0), (d, 1))]

        def up(h):
            return whole(-2 * h)

        def side(h):
            return side_both(h) + whole(1 - 2 * k - 2 * h)

        def both_up(part):
            return [((-2 * (last - 1), part), (-2 * last, part))]

        def both_side(part):
            d = 1 - 2 * k
            return [("side", last - 1, part), ("side", last, part), ((d - 2 * (last - 1), part), (d - 2 * last, part))]

        start = [("queries",)] + whole(0)
        relays = [[("relay", g)] for g in wrapped] + [[]] * 4
        if c == 0:
            return start + (side(0) if k == 1 else []) + [("straight",)]
        if c == 1 and k == 0:
            return ([("take", 1, 0)] + start + relays[0] + [("take", 1, 1)] + relays[1] + side(1) + relays[2] + relays[3]
                    + up(1))
        if c == 1:
            return (take_both(1) + start + relays[0] + up(1) + relays[1] + side(0) + relays[2] + relays[3] + side(1))
        if c == 2 and k == 0:
            return ([("take", 1, 0)] + start + side(1) + [("take", 1, 1)] + up(1) + side(2) + take_both(2) + up(2))
        if c == 2:
            return take_both(1) + start + up(1) + side(0) + take_both(2) + up(2) + side(1) + side(2)
        if k == 0:
            return ([("take", 1, 0)] + start + side(1) + [("take", 1, 1)] + up(1)
                    + [("take", 2, 0)] + side(2) + [("take", 3, 0)] + both_up(0)
                    + side(3) + [("take", 2, 1), ("take", 3, 1)]
                    + both_up(1))
        return (take_both(1) + start + up(1) + side(0) + take_both(2) + up(2) + side(1) + take_both(3) + up(3)
                + both_side(0) + both_side(1))

    def run(c, k):
        steps, waits = [], []
        for one in plan(c, k):
            if isinstance(one[0], str):
                waits.append(one)
            else:
                steps.append((waits, one))
                waits = []

        @pl.loop(0, len(steps))
        def _(i):
            pieces = [[jnp.int32(0), jnp.int32(0)], [jnp.int32(0), jnp.int32(0)]]
            for n, (before, pair) in enumerate(steps):

                @pl.when(i == n)
                def _():
                    for one in before:
                        do(*one)

                for piece, (distance, part) in zip(pieces, pair):
                    piece[0] = jnp.where(i == n, distance, piece[0])
                    piece[1] = jnp.where(i == n, part, piece[1])
            absorb(*((span + distance, part) for distance, part in pieces))

        for one in waits:
            do(*one)

    for c in range(n_chip):
        for k in range(2):
            pl.when((chip == c) & (core == k))(functools.partial(run, c, k))

    for g in list(range(2, n_g)) + [1, 0]:
        at = slice(g * rows, (g + 1) * rows)
        whole = jnp.sum(total[at, : min(HD, n_g * rows)], axis=-1, keepdims=True)
        obuf[at, :] = (accum[at, :] * (1.0 / whole) * gate_row[0:1, :]).astype(jnp.bfloat16)
        for s, _, _ in far_first:
            if s // per == g:
                pltpu.make_async_remote_copy(
                    src_ref=obuf.at[s * tok : (s + 1) * tok, :],
                    dst_ref=out_ref.at[0, :, pl.ds(pl.multiple_of(seq * HD, HD), HD)],
                    send_sem=o_send,
                    recv_sem=o_recv,
                    device_id={"seq": behind[s]},
                ).start()
    mine = pltpu.make_async_copy(
        obuf.at[0:tok, :], out_ref.at[0, :, pl.ds(pl.multiple_of(seq * HD, HD), HD)], in_sem.at[0]
    )
    mine.start()
    mine.wait()

    def drain(ref, sem):
        pltpu.make_async_copy(ref, ref, sem).wait()

    drain(kv_stage.at[1:n_seq], kv_send)
    drain(q_stage.at[1:n_seq], q_send)
    pl.when(chip < last)(functools.partial(drain, kv_stage.at[0:per], direct_send))
    for c in range(n_chip):
        passed = [h for h in range(c + 1) if not (wrap and h == last - 1)] if c < last else []
        n_down = len(passed) * n_g - (n_direct if c < last else 0)
        n_down += len(straight) if c == 0 else 0
        if n_down:
            pl.when(chip == c)(functools.partial(drain, kv.at[0:n_down], down_send))
        pl.when((chip == c) & (core == 0))(functools.partial(drain, kv.at[0 : (c + 1) * n_g], side_send))
        if c > 0:
            pl.when((chip == c) & (core == 1))(functools.partial(drain, kv.at[0 : c * n_g], side_send))
    if wrap:
        if len(wrapped):
            pl.when(chip == 0)(functools.partial(drain, relay.at[0 : len(wrapped)], wrap_send))
            pl.when(chip == 1)(functools.partial(drain, relay.at[0 : len(wrapped)], relay_send))
        pl.when(chip == 0)(functools.partial(drain, kv_stage.at[0:per], far_send))
    drain(obuf.at[tok:, :], o_send)
    drain(out_ref.at[0, :, 0 : (n_seq - 1) * HD], o_recv)


def body(queries, keys, values, timesteps, history, gate_weight):
    n_span, n_seq = lax.axis_size("span"), lax.axis_size("seq")
    n_x = 4 if n_seq == 32 else 2
    n_z = n_seq // n_x
    n_g = GN if n_seq == 32 else 2
    wrap = n_span == 8 and lax.axis_size("rep") == 2
    tok, width = queries.shape[1], queries.shape[2]
    bf16, f32 = jnp.bfloat16, jnp.float32
    rows = n_seq // n_g * tok
    whole = n_seq * tok
    return pl.pallas_call(
        functools.partial(kernel, n_span, n_x, n_z, n_g, wrap, tok),
        out_shape=pltpu.VMEM(queries.shape, bf16),
        in_specs=[pl.BlockSpec(memory_space=pl.ANY)] * 6,
        out_specs=pl.BlockSpec(memory_space=pltpu.VMEM),
        scratch_shapes=[
            pltpu.VMEM((tok, width), bf16),
            pltpu.VMEM((tok, width), bf16),
            pltpu.VMEM((tok, width), bf16),
            pltpu.SMEM(timesteps.shape, timesteps.dtype),
            pltpu.VMEM(history.shape, history.dtype),
            pltpu.VMEM(gate_weight.shape, bf16),
            pltpu.VMEM((n_seq, 2, tok, HD), bf16),
            pltpu.VMEM((n_seq, tok, HD), bf16),
            pltpu.VMEM((n_span * n_g, 2, rows, HD), bf16),
            pltpu.VMEM((n_g, 2, rows, HD), bf16),
            pltpu.VMEM((whole, HD), bf16),
            pltpu.VMEM((whole, HD), bf16),
            pltpu.VMEM((2, n_span, whole // 2), f32),
            pltpu.VMEM((8, HD), f32),
            pltpu.VMEM((whole, HD), f32),
            pltpu.VMEM((whole, HD), f32),
            pltpu.VMEM((whole, HD), f32),
            pltpu.SemaphoreType.DMA((6,)),
            pltpu.SemaphoreType.DMA((n_span * n_g,)),
            pltpu.SemaphoreType.DMA,
            pltpu.SemaphoreType.DMA,
            pltpu.SemaphoreType.DMA,
            pltpu.SemaphoreType.DMA,
            pltpu.SemaphoreType.DMA,
            pltpu.SemaphoreType.DMA,
            pltpu.SemaphoreType.DMA,
            pltpu.SemaphoreType.DMA,
            pltpu.SemaphoreType.DMA((n_g,)),
            pltpu.SemaphoreType.DMA,
            pltpu.SemaphoreType.DMA,
            pltpu.SemaphoreType.DMA,
        ],
        compiler_params=pltpu.CompilerParams(
            collective_id=0, has_side_effects=True, vmem_limit_bytes=VLIM * 2**20
        ),
        name="attention",
    )(queries, keys, values, timesteps, history, gate_weight)


def solution(mesh):
    return jax.shard_map(
        body,
        mesh=mesh,
        in_specs=(
            P(("rep", "span"), "seq", None),
            P(("rep", "span"), "seq", None),
            P(("rep", "span"), "seq", None),
            P(("rep", "span")),
            P(("rep", "span"), None),
            P(None, "seq"),
        ),
        out_specs=P(("rep", "span"), "seq", None),
        check_vma=False,
    )
```
